768 devices in a mesh: lon: 16 (over y, z_hi), lat: 48 (over z_lo, x, core).
Axes of the slice: x: 4, y: 8, z: 12 (z_hi: 2, z_lo: 6; z = z_hi * 6 + z_lo), core: 2. Of those that a mesh axis runs over, the one named last changes fastest.
Arguments:
- gradient: float32 [2, 768, 4096], P(None, 'lat', 'lon'), may hold values from -6 to 6
- norm_factor: float32 [2, 768, 4096], P(None, 'lat', 'lon'), may hold values from 0.5 to 4
- diff_east: float32 [2, 768, 4096], P(None, 'lat', 'lon'), may hold values from 0.02 to 0.25
- diff_north: float32 [2, 768, 4096], P(None, 'lat', 'lon'), may hold values from 0.02 to 0.25
- cell_area: float32 [768, 4096], P('lat', 'lon'), may hold values from 1 to 2.5
- sea_mask: int32 [768, 4096], P('lat', 'lon'), may hold values 0 or 1
- partner: int32 [4096], replicated, may hold values from 0 to 4095, as said below
Outputs:
- adjoint_field: float32 [2, 768, 4096], P(None, 'lat', 'lon')
The draws below stay inside these ranges and needn't reach their ends.
Inputs may be any that keep to these rules, and one draw needn't show every extreme that they name: partner is a reflection of the columns: partner[j] = (c - j) modulo 4096 for one column c, so partner[partner[j]] = j.
All inputs are finite; a program needn't handle non-finite values. No bound on the sum of `sea_mask` on one device may be relied on, other than what follows from the above.
Results may differ from the reference program's by a relative error of at most 0.00002.
Values sent between devices are 32-bit elements; how exact they have to be, the bound alone decides.
No kernel may reach another device: no remote copies, remote signals or barrier semaphores. Data moves between devices by JAX's collectives and lax.ppermute only.
A program may use at most 128 MiB of HBM per device.

```python
import math
import jax
import jax.numpy as jnp
from jax import lax

LEV = 2
ITERS = 10
NLAT = 768
NLON = 4096


def draw_partner(key, part):
    key = jax.random.fold_in(key, 7)
    centre = jax.random.randint(key, (), 0, NLON)
    return ((centre - jnp.arange(NLON, dtype=jnp.int32)) % NLON).astype(jnp.int32)


def plant(drawn, own_key, low, top_value):
    place = [jax.random.randint(jax.random.fold_in(own_key, axis), (), 0, length) for axis, length in enumerate(drawn.shape)]
    widest = drawn.shape.index(max(drawn.shape))
    beside = place[:widest] + [(place[widest] + 1) % drawn.shape[widest]] + place[widest + 1:]
    return drawn.at[tuple(place)].set(low).at[tuple(beside)].set(top_value)


def shard_levels(stream_key, shape, pieces, least, high):
    gain, own = 1.0, jax.random.fold_in(stream_key, 6)
    for axis_at, parts in pieces:
        draws = jnp.exp(jax.random.uniform(jax.random.fold_in(own, axis_at), (parts,), jnp.float32, least / len(pieces), high / len(pieces)))
        gain = gain * jnp.repeat(draws, shape[axis_at] // parts).reshape([-1 if axis == axis_at else 1 for axis in range(len(shape))])
    return gain


def gaussian(rng, shape, width, bound, shards=(), held_as=jnp.bfloat16):
    result = width * jax.random.normal(rng, shape, jnp.float32)
    if shards:
        result = result * shard_levels(rng, shape, shards, -0.22, 0.18)
    return jnp.clip(result, -bound, bound).astype(held_as)


def setup_inputs(seed: int = 0) -> dict:
    arg_keys = jax.random.split(jax.random.key(seed), 8)
    gradient = gaussian(arg_keys[0], (LEV, NLAT, NLON), 1.0, 6.0, ((1, 48), (2, 16)), jnp.float32)
    norm_factor = jnp.clip(jnp.exp(math.log(4.0) - 2.0794415 * jax.random.uniform(arg_keys[1], (LEV, NLAT, NLON), jnp.float32) ** shard_levels(arg_keys[1], (LEV, NLAT, NLON), ((1, 48), (2, 16)), -0.2, 0.2)), 0.5, 4.0)
    diff_east = jnp.clip(0.02 + 0.23 * jax.random.uniform(arg_keys[2], (LEV, NLAT, NLON), jnp.float32) ** shard_levels(arg_keys[2], (LEV, NLAT, NLON), ((1, 48), (2, 16)), -0.2, 0.2), 0.02, 0.25)
    diff_north = jnp.clip(0.02 + 0.23 * jax.random.uniform(arg_keys[3], (LEV, NLAT, NLON), jnp.float32) ** shard_levels(arg_keys[3], (LEV, NLAT, NLON), ((1, 48), (2, 16)), -0.2, 0.2), 0.02, 0.25)
    cell_area = jnp.clip(jnp.exp(math.log(2.5) - 0.916290732 * jax.random.uniform(arg_keys[4], (NLAT, NLON), jnp.float32) ** shard_levels(arg_keys[4], (NLAT, NLON), ((0, 48), (1, 16)), -0.2, 0.2)), 1.0, 2.5)
    sea_mask = plant((jax.random.randint(arg_keys[5], (NLAT, NLON), 0, 4) < 3).astype(jnp.int32), jax.random.fold_in(arg_keys[5], 1), 0, 1)
    partner = draw_partner(jax.random.fold_in(arg_keys[7], 71), 0)
    return {"gradient": gradient, "norm_factor": norm_factor, "diff_east": diff_east, "diff_north": diff_north, "cell_area": cell_area, "sea_mask": sea_mask, "partner": partner}


def neighbours(source, partner):
    east = jnp.roll(source, -1, 1)
    west = jnp.roll(source, 1, 1)
    south = jnp.concatenate([jnp.zeros_like(source[:1]), source[:-1]], 0)
    north = jnp.concatenate([source[1:], source[-1:][:, partner]], 0)
    return (east, west, south, north)

def reference(gradient, norm_factor, diff_east, diff_north, cell_area, sea_mask, partner):
    ocean = sea_mask.astype(jnp.float32)
    ocean_east, ocean_west, ocean_south, ocean_north = neighbours(ocean, partner)
    row_index = lax.broadcasted_iota(jnp.int32, (NLAT, NLON), 0)
    at_top = row_index == NLAT - 1

    def level(inputs):
        grad_level, factor, east_diff, north_diff = inputs
        east_coef = east_diff * ocean * ocean_east
        west_coef = jnp.roll(east_diff, 1, 1) * ocean_west * ocean
        unused_east, unused_west, north_south, north_fold = neighbours(north_diff, partner)
        north_coef = jnp.where(at_top, 0.5 * (north_diff + north_fold), north_diff) * ocean * ocean_north
        south_coef = north_south * ocean_south * ocean

        def advance(turn, current):
            weighted = ocean * current / cell_area
            w_east, w_west, w_south, w_north = neighbours(weighted, partner)
            return current + east_coef * (w_east - weighted) + west_coef * (w_west - weighted) + north_coef * (w_north - weighted) + south_coef * (w_south - weighted)
        current = lax.fori_loop(0, ITERS, advance, factor * grad_level)
        return current / jnp.sqrt(cell_area)
    return lax.map(level, (gradient, norm_factor, diff_east, diff_north))
```

```python
import jax
import jax.numpy as jnp
from jax import lax
from jax.experimental import pallas as pl
from jax.experimental.pallas import tpu as pltpu
from jax.sharding import PartitionSpec as P

ITERS = 10
LANES = 128
TILE = 8
AXES = ("lon", "lat")


def pack_kernel(grad, norm, de, dn, area, mask, packed):
    levels = grad.shape[0]
    packed[0:levels] = norm[...] * grad[...]
    packed[levels : 2 * levels] = de[...]
    packed[2 * levels : 3 * levels] = dn[...]
    packed[3 * levels] = mask[...].astype(jnp.float32) / area[...]


def reversed_lanes(x):
    index = LANES - 1 - lax.broadcasted_iota(jnp.int32, (x.shape[0], LANES), 1)
    pieces = []
    for start in range(x.shape[1] - LANES, -1, -LANES):
        piece = x[:, start : start + LANES]
        pieces.append(jnp.take_along_axis(piece, index, axis=1, mode="promise_in_bounds"))
    return pieces


def halo_slots(arrays, tiles):
    per_row = LANES // ITERS
    places = [(k, t) for k in range(arrays) for t in range(tiles)]
    return [(k, t, m // per_row, (m % per_row) * ITERS) for m, (k, t) in enumerate(places)]


def grow_kernel(lat_count, levels, centre, own, upward, downward, last, grown, to_east, to_west):
    arrays, rows, cols = own.shape
    lat_place = lax.axis_index("lat")
    top = lat_count - 1
    grown[:, rows : 2 * rows] = own[...]

    @pl.when(lat_place < top)
    def _():
        grown[:, 0:rows] = upward[...]

    @pl.when(lat_place < top - 1)
    def _():
        grown[:, 2 * rows : 3 * rows] = downward[...]

    @pl.when(lat_place == top - 1)
    def _():
        grown[:, 2 * rows : 3 * rows] = last[...]

    @pl.when(lat_place == top)
    def _():
        grown[:, 0:rows] = last[...]
        offset = lax.rem(centre[0], cols)
        for k in range(arrays):
            east_face = levels <= k < 2 * levels
            north_face = 2 * levels <= k < 3 * levels
            wide = jnp.concatenate(reversed_lanes(upward[k]) + reversed_lanes(downward[k]), axis=1)
            shift = offset + (cols if east_face else cols + 1)
            mirrored = pltpu.roll(wide, shift, 1)[:, :cols]
            if north_face:
                face = own[k, rows - 1 : rows]
                grown[k, 2 * rows - 1 : 2 * rows] = 0.5 * (face + mirrored[rows - 1 : rows])
            skip = 1 if north_face else 0
            for row in range(rows):
                source = max(rows - 1 - skip - row, 0)
                grown[k, 2 * rows + row : 2 * rows + row + 1] = mirrored[source : source + 1]

    row_index = lax.broadcasted_iota(jnp.int32, (TILE, LANES), 0)
    lane = lax.broadcasted_iota(jnp.int32, (TILE, LANES), 1)
    tiles = 3 * rows // TILE

    def piece(k, t, col):
        def tile(at):
            return grown[k, at * TILE : (at + 1) * TILE, col : col + LANES]

        if t == 0:
            return jnp.where(row_index == TILE - 1, tile(0), tile(tiles - 1))
        return tile(t)

    for out, col, first in ((to_east, cols - LANES, LANES - ITERS), (to_west, 0, 0)):
        held = {}
        for k, t, row, place in halo_slots(arrays, tiles - 1):
            moved = pltpu.roll(piece(k, t, col), (place - first) % LANES, 1)
            inside = (lane >= place) & (lane < place + ITERS)
            held[row] = jnp.where(inside, moved, held.get(row, jnp.zeros_like(moved)))
        for row, value in held.items():
            out[row * TILE : (row + 1) * TILE] = value


def steps_kernel(levels, grown, from_east, from_west, area, out):
    arrays, tall, cols = grown.shape
    rows = tall // 3
    tiles = tall // TILE
    lane = lax.broadcasted_iota(jnp.int32, (TILE, LANES), 1)
    edge = {}
    for k, t, row, place in halo_slots(arrays, tiles - 1):
        rows_held = slice(row * TILE, (row + 1) * TILE)
        east = pltpu.roll(from_east[rows_held], (-place) % LANES, 1)
        west = pltpu.roll(from_west[rows_held], (LANES - ITERS - place) % LANES, 1)
        edge[k, t] = jnp.where(lane < ITERS, east, jnp.where(lane >= LANES - ITERS, west, 0.0))

    def whole(k):
        side = jnp.concatenate([edge[k, t % (tiles - 1)] for t in range(tiles)], axis=0)
        return jnp.concatenate([grown[k], side], axis=1)

    wide = cols + LANES

    def east_of(x):
        return pltpu.roll(x, wide - 1, 1)

    def west_of(x):
        return pltpu.roll(x, 1, 1)

    def north_of(x):
        return pltpu.roll(x, x.shape[0] - 1, 0)

    def south_of(x):
        return pltpu.roll(x, 1, 0)

    weight = whole(3 * levels)
    sea = jnp.where(weight > 0.0, 1.0, 0.0)
    sea_pair_east = sea * east_of(sea)
    sea_pair_north = sea * north_of(sea)
    root = jnp.sqrt(area[...])
    for level in range(levels):
        state = whole(level)
        east_face = whole(levels + level) * sea_pair_east
        north_face = whole(2 * levels + level) * sea_pair_north
        held = weight
        for turn in range(ITERS):
            weighted = held * state
            east_flow = east_face * (east_of(weighted) - weighted)
            north_flow = north_face * (north_of(weighted) - weighted)
            state = state + ((east_flow - west_of(east_flow)) + (north_flow - south_of(north_flow)))
            if turn == 1:
                inner = slice(TILE, tall - TILE)
                state, held = state[inner], held[inner]
                east_face, north_face = east_face[inner], north_face[inner]
        start = rows - TILE
        out[level] = state[start : start + rows, :cols] / root


def vmem(count):
    return [pl.BlockSpec(memory_space=pltpu.VMEM)] * count


def per_device(gradient, norm_factor, diff_east, diff_north, cell_area, sea_mask, partner):
    levels, rows, cols = gradient.shape
    arrays = 3 * levels + 1
    lon_count, lat_count = lax.axis_size("lon"), lax.axis_size("lat")
    centre = partner[:1]
    f32 = jnp.float32
    block = jax.ShapeDtypeStruct((arrays, rows, cols), f32)
    packed = pl.pallas_call(
        pack_kernel, out_shape=block, in_specs=vmem(6), out_specs=vmem(1)[0]
    )(gradient, norm_factor, diff_east, diff_north, cell_area, sea_mask)

    def flat(lon, lat):
        return (lon % lon_count) * lat_count + lat

    top = lat_count - 1
    places = range(lon_count)
    north_going = [(flat(p, i), flat(p, i + 1)) for p in places for i in range(top - 1)]
    south_going = [(b, a) for a, b in north_going]
    last_north = [(flat(p, top - 1), flat(p, top)) for p in places]
    last_south = [(b, a) for a, b in last_north]

    def mirror(block_sum):
        return [(flat(block_sum - p, top), flat(p, top)) for p in places]

    def exchange(block_sum):
        def run(x):
            upward = lax.ppermute(x, AXES, north_going + mirror(block_sum))
            downward = lax.ppermute(x, AXES, south_going + mirror(block_sum - 1))
            return upward, downward

        return run

    last = lax.ppermute(packed, AXES, last_north + last_south)
    upward, downward = lax.switch(
        centre[0] // cols, [exchange(k) for k in places], packed
    )
    slots = halo_slots(arrays, 3 * rows // TILE - 1)
    edge = jax.ShapeDtypeStruct(((slots[-1][2] + 1) * TILE, LANES), f32)

    def grow(*refs):
        grow_kernel(lat_count, levels, *refs)

    grown, to_east, to_west = pl.pallas_call(
        grow,
        out_shape=(jax.ShapeDtypeStruct((arrays, 3 * rows, cols), f32), edge, edge),
        in_specs=[pl.BlockSpec(memory_space=pltpu.SMEM)] + vmem(4),
        out_specs=tuple(vmem(3)),
    )(centre, packed, upward, downward, last)
    east_going = [(p, (p + 1) % lon_count) for p in range(lon_count)]
    from_west = lax.ppermute(to_east, "lon", east_going)
    from_east = lax.ppermute(to_west, "lon", [(b, a) for a, b in east_going])

    def steps(*refs):
        steps_kernel(levels, *refs)

    return pl.pallas_call(
        steps,
        out_shape=jax.ShapeDtypeStruct((levels, rows, cols), f32),
        in_specs=vmem(4),
        out_specs=vmem(1)[0],
    )(grown, from_east, from_west, cell_area)


def solution(mesh):
    return jax.shard_map(
        per_device,
        mesh=mesh,
        in_specs=(
            P(None, "lat", "lon"),
            P(None, "lat", "lon"),
            P(None, "lat", "lon"),
            P(None, "lat", "lon"),
            P("lat", "lon"),
            P("lat", "lon"),
            P(),
        ),
        out_specs=P(None, "lat", "lon"),
        check_vma=False,
    )
```

```python
import jax
import jax.numpy as jnp
from jax import lax
from jax.experimental import pallas as pl
from jax.experimental.pallas import tpu as pltpu
from jax.sharding import PartitionSpec as P

ITERS = 10
LANES = 128
TILE = 8
PER_ROW = LANES // ITERS
AXES = ("lon", "lat")


def lane_index(rows=TILE):
    return lax.broadcasted_iota(jnp.int32, (rows, LANES), 1)


def slots(arrays):
    places = [(k, t) for k in range(arrays) for t in range(2)]
    return [(k, t, m // PER_ROW, (m % PER_ROW) * ITERS) for m, (k, t) in enumerate(places)]


def pack_kernel(partner, grad, norm, de, dn, area, mask, block, edges, x_rows, y_rows, place, held, arrived):
    levels, rows, cols = grad.shape
    arrays = block.shape[0]
    copy = pltpu.make_async_copy(partner.at[pl.ds(0, held.shape[0])], held, arrived)
    copy.start()
    block[0:levels] = norm[...] * grad[...]
    block[levels : 2 * levels] = de[...]
    block[2 * levels : 3 * levels] = dn[...]
    block[3 * levels] = mask[...].astype(jnp.float32) / area[...]
    lane = lane_index()
    lon_even = lax.rem(lax.axis_index("lon"), 2) == 0
    lat_even = lax.rem(lax.axis_index("lat"), 2) == 0

    def packed(col, first):
        out = {}
        for k, t, row, at in slots(arrays):
            tile = block[k, t * TILE : (t + 1) * TILE, col : col + LANES]
            moved = pltpu.roll(tile, (at - first) % LANES, 1)
            inside = (lane >= at) & (lane < at + ITERS)
            out[row] = jnp.where(inside, moved, out.get(row, jnp.zeros_like(moved)))
        return out

    east, west = packed(cols - LANES, LANES - ITERS), packed(0, 0)
    count = len(east)
    for row in range(count):
        here = slice(row * TILE, (row + 1) * TILE)
        there = slice((count + row) * TILE, (count + row + 1) * TILE)
        edges[here] = jnp.where(lon_even, east[row], west[row])
        edges[there] = jnp.where(lon_even, west[row], east[row])

    sub = lax.broadcasted_iota(jnp.int32, (TILE, LANES), 0)
    for c in range(cols // LANES):
        at = slice(c * LANES, (c + 1) * LANES)
        base = c * (arrays + 2) * TILE
        extra = {}
        for k in range(arrays):
            low, high = block[k, 0:TILE, at], block[k, TILE : 2 * TILE, at]
            here = slice(base + k * TILE, base + (k + 1) * TILE)
            x_rows[here] = jnp.where(lat_even, high, low)
            y_rows[here] = jnp.where(lat_even, low, high)
            lift = 2 * (k % 4)
            inside = (sub >= lift) & (sub < lift + 2)
            north = pltpu.roll(low, (lift + 2) % TILE, 0)
            south = pltpu.roll(high, lift, 0)
            north_held, south_held = extra.get(k // 4, (jnp.zeros_like(low),) * 2)
            extra[k // 4] = (jnp.where(inside, north, north_held), jnp.where(inside, south, south_held))
        for e, (north, south) in extra.items():
            here = slice(base + (arrays + e) * TILE, base + (arrays + e + 1) * TILE)
            x_rows[here] = jnp.where(lat_even, north, south)
            y_rows[here] = jnp.where(lat_even, south, north)
    copy.wait()
    moved = held[0] + ITERS
    q = lax.rem(lax.div(moved, cols), lax.axis_size("lon"))
    offset = lax.rem(moved, cols) - ITERS
    place[0] = 2 * q + jnp.where(offset < ITERS - 1, 1, 0)
    place[1] = offset


def near_kernel(x_rows, y_rows, first, second, after, x_out, y_out):
    del after
    rows, tall = x_rows.shape[0], first.shape[0]
    half = tall // 2
    x_out[0:rows] = x_rows[...]
    x_out[rows : rows + tall] = first[...]
    x_out[rows + tall : rows + 2 * tall] = second[...]
    y_out[0:rows] = y_rows[...]
    y_out[rows : rows + half] = first[0:half]
    y_out[rows + half : rows + tall] = second[0:half]


def reversed_lanes(x):
    index = LANES - 1 - lane_index(x.shape[0])
    return jnp.take_along_axis(x, index, axis=1, mode="promise_in_bounds")


def steps_kernel(levels, place, own, first, second, x_in, y_in, f0, f1, f2, area, out, ext):
    arrays, rows, cols = own.shape
    wide, tall = cols + LANES, 3 * rows
    tiles_across = cols // LANES
    band = (arrays + 2) * TILE
    data = band * tiles_across
    edge = first.shape[0] // 2
    lon_even = lax.rem(lax.axis_index("lon"), 2) == 0
    lat = lax.axis_index("lat")
    lat_even = lax.rem(lat, 2) == 0
    at_top = lat == lax.axis_size("lat") - 1
    below_top = lat == lax.axis_size("lat") - 2
    lane = lane_index()

    def put_sides(start, a, b):
        from_east, from_west = jnp.where(lon_even, a, b), jnp.where(lon_even, b, a)
        for k, t, row, at in slots(arrays):
            here = slice(row * TILE, (row + 1) * TILE)
            east = pltpu.roll(from_east[here], (-at) % LANES, 1)
            west = pltpu.roll(from_west[here], (LANES - ITERS - at) % LANES, 1)
            side = jnp.where(lane < ITERS, east, jnp.where(lane >= LANES - ITERS, west, 0.0))
            ext[k, start + t * TILE : start + (t + 1) * TILE, cols:wide] = side

    def put_rows(start, main, spare, lift_base, rows_of):
        for c in range(tiles_across):
            at = slice(c * LANES, (c + 1) * LANES)
            for k in range(arrays):
                base = c * band
                ext[k, start + main * TILE : start + (main + 1) * TILE, at] = rows_of(base + k * TILE)
                few = rows_of(base + (arrays + k // 4) * TILE)
                lift = (lift_base - 2 * (k % 4)) % TILE
                ext[k, start + spare * TILE : start + (spare + 1) * TILE, at] = pltpu.roll(few, lift, 0)

    for k in range(arrays):
        ext[k, rows : 2 * rows, 0:cols] = own[k]
    x_first, x_second = x_in[data : data + edge], x_in[data + 2 * edge : data + 3 * edge]
    x_mate_first, x_mate_second = x_in[data + edge : data + 2 * edge], x_in[data + 3 * edge : data + 4 * edge]
    y_first, y_second = y_in[data : data + edge], y_in[data + edge : data + 2 * edge]
    put_sides(
        rows,
        jnp.where(at_top, x_mate_first, first[0:edge]),
        jnp.where(at_top, x_mate_second, second[0:edge]),
    )

    def south_rows(at):
        return jnp.where(lat_even, y_in[at : at + TILE], x_in[at : at + TILE])

    def north_rows(at):
        return jnp.where(lat_even, x_in[at : at + TILE], y_in[at : at + TILE])

    put_rows(0, 1, 0, TILE - 2, south_rows)
    put_sides(0, jnp.where(lat_even, y_first, x_first), jnp.where(lat_even, y_second, x_second))

    @pl.when(jnp.logical_not(at_top))
    def _():
        put_rows(2 * rows, 0, 1, 0, north_rows)
        put_sides(
            2 * rows,
            jnp.where(below_top, first[edge : 2 * edge], jnp.where(lat_even, x_first, y_first)),
            jnp.where(below_top, second[edge : 2 * edge], jnp.where(lat_even, x_second, y_second)),
        )

    @pl.when(at_top)
    def _():
        offset = place[1]
        span = 3 * cols
        for k in range(arrays):
            east_face = levels <= k < 2 * levels
            north_face = 2 * levels <= k < 3 * levels
            pieces = []
            for f in (f0, f1, f2):
                for c in range(tiles_across - 1, -1, -1):
                    main = f[c * band + k * TILE : c * band + (k + 1) * TILE]
                    few = f[c * band + (arrays + k // 4) * TILE : c * band + (arrays + k // 4 + 1) * TILE]
                    few = pltpu.roll(few, (TILE - 2 - 2 * (k % 4)) % TILE, 0)
                    pieces.append(reversed_lanes(jnp.concatenate([few, main], axis=0)))
            shift = offset + span - cols + (0 if east_face else 1)
            turned = pltpu.roll(jnp.concatenate(pieces, axis=1), shift, 1)
            far = lane_index(rows)
            beyond = turned[:, cols : cols + LANES]
            before = turned[:, span - LANES :]
            side = jnp.where(far < ITERS, beyond, jnp.where(far >= LANES - ITERS, before, 0.0))
            mirrored = jnp.concatenate([turned[:, :cols], side], axis=1)
            if north_face:
                face = ext[k, 2 * rows - 1 : 2 * rows]
                ext[k, 2 * rows - 1 : 2 * rows] = 0.5 * (face + mirrored[rows - 1 : rows])
            skip = 1 if north_face else 0
            for row in range(rows):
                source = max(rows - 1 - skip - row, 0)
                ext[k, 2 * rows + row : 2 * rows + row + 1] = mirrored[source : source + 1]

    def east_of(x):
        return pltpu.roll(x, wide - 1, 1)

    def west_of(x):
        return pltpu.roll(x, 1, 1)

    def north_of(x):
        return pltpu.roll(x, x.shape[0] - 1, 0)

    def south_of(x):
        return pltpu.roll(x, 1, 0)

    weight = ext[3 * levels]
    sea = jnp.where(weight > 0.0, 1.0, 0.0)
    sea_east = sea * east_of(sea)
    sea_north = sea * north_of(sea)
    root = jnp.sqrt(area[...])
    for level in range(levels):
        state = ext[level]
        east_face = ext[levels + level] * sea_east
        north_face = ext[2 * levels + level] * sea_north
        held = weight
        for turn in range(ITERS):
            weighted = held * state
            east_flow = east_face * (east_of(weighted) - weighted)
            north_flow = north_face * (north_of(weighted) - weighted)
            state = state + ((east_flow - west_of(east_flow)) + (north_flow - south_of(north_flow)))
            if turn == 1:
                inner = slice(TILE, tall - TILE)
                state, held = state[inner], held[inner]
                east_face, north_face = east_face[inner], north_face[inner]
        start = rows - TILE
        out[level] = state[start : start + rows, :cols] / root


VMEM = pl.BlockSpec(memory_space=pltpu.VMEM)
SMEM = pl.BlockSpec(memory_space=pltpu.SMEM)
ANY = pl.BlockSpec(memory_space=pl.ANY)
PARAMS = pltpu.CompilerParams(vmem_limit_bytes=8 * 1024 * 1024)


def per_device(gradient, norm_factor, diff_east, diff_north, cell_area, sea_mask, partner):
    levels, rows, cols = gradient.shape
    arrays = 3 * levels + 1
    lon_count, lat_count = lax.axis_size("lon"), lax.axis_size("lat")

    def held(*shape):
        return jax.ShapeDtypeStruct(shape, jnp.float32)

    edge = (slots(arrays)[-1][2] + 1) * TILE
    data = (arrays + 2) * TILE * (cols // LANES)
    block, edges, x_rows, y_rows, place = pl.pallas_call(
        pack_kernel,
        out_shape=(
            held(arrays, rows, cols),
            held(2 * edge, LANES),
            held(data, LANES),
            held(data, LANES),
            jax.ShapeDtypeStruct((2,), jnp.int32),
        ),
        in_specs=[ANY] + [VMEM] * 6,
        out_specs=(VMEM, VMEM, VMEM, VMEM, SMEM),
        scratch_shapes=[pltpu.SMEM((LANES,), jnp.int32), pltpu.SemaphoreType.DMA],
        compiler_params=PARAMS,
    )(partner, gradient, norm_factor, diff_east, diff_north, cell_area, sea_mask)

    def flat(lon, lat):
        return (lon % lon_count) * lat_count + lat

    top = lat_count - 1
    around = range(lon_count)

    def swap(pairs):
        return [pair for a, b in pairs for pair in ((a, b), (b, a))]

    def lon_swap(start):
        return swap([(flat(p, i), flat(p + 1, i)) for p in around[start::2] for i in range(top)])

    def lat_swap(start):
        return swap([(flat(p, i), flat(p, i + 1)) for p in around for i in range(start, top, 2)])

    def mirror(total):
        return [(flat(total - p, top), flat(p, top)) for p in around]

    mate = lax.ppermute(edges, AXES, [(flat(p, top), flat(p, top - 1)) for p in around])
    first = lax.ppermute(jnp.concatenate([edges[:edge], mate[:edge]]), AXES, lon_swap(0))
    second = lax.ppermute(jnp.concatenate([edges[edge:], mate[edge:]]), AXES, lon_swap(1))

    def fold(total, third):
        def run(x):
            f0 = lax.ppermute(x, AXES, mirror(total))
            f1 = lax.ppermute(x, AXES, mirror(total - 1))
            f2 = lax.ppermute(x, AXES, mirror(total - 2)) if third else jnp.zeros_like(x)
            return f0, f1, f2

        return run

    branches = [fold(total, third) for total in around for third in (False, True)]
    f0, f1, f2 = lax.switch(place[0], branches, y_rows)
    x_out, y_out = pl.pallas_call(
        near_kernel,
        out_shape=(held(data + 4 * edge, LANES), held(data + 2 * edge, LANES)),
        in_specs=[VMEM] * 4 + [ANY],
        out_specs=(VMEM, VMEM),
        compiler_params=PARAMS,
    )(x_rows, y_rows, first, second, f0)
    x_in = lax.ppermute(x_out, AXES, lat_swap(0))
    y_in = lax.ppermute(y_out, AXES, lat_swap(1))

    def steps(*refs):
        steps_kernel(levels, *refs)

    return pl.pallas_call(
        steps,
        out_shape=held(levels, rows, cols),
        in_specs=[SMEM] + [VMEM] * 9,
        out_specs=VMEM,
        scratch_shapes=[pltpu.VMEM((arrays, 3 * rows, cols + LANES), jnp.float32)],
        compiler_params=PARAMS,
    )(place, block, first, second, x_in, y_in, f0, f1, f2, cell_area)


def solution(mesh):
    return jax.shard_map(
        per_device,
        mesh=mesh,
        in_specs=(
            P(None, "lat", "lon"),
            P(None, "lat", "lon"),
            P(None, "lat", "lon"),
            P(None, "lat", "lon"),
            P("lat", "lon"),
            P("lat", "lon"),
            P(),
        ),
        out_specs=P(None, "lat", "lon"),
        check_vma=False,
    )
```

```python
import functools

import jax
import jax.numpy as jnp
from jax import lax
from jax.experimental import pallas as pl
from jax.experimental.pallas import tpu as pltpu
from jax.sharding import PartitionSpec as P

ITERS = 10
LANES = 128
TILE = 8
PER_ROW = LANES // ITERS
AXES = ("lon", "lat")


def lane_index(rows=TILE):
    return lax.broadcasted_iota(jnp.int32, (rows, LANES), 1)


def slots(arrays):
    places = [(k, t) for k in range(arrays) for t in range(2)]
    return [(k, t, m // PER_ROW, (m % PER_ROW) * ITERS) for m, (k, t) in enumerate(places)]


def pack_kernel(*refs):
    sources, (block, edges, x_rows, y_rows, area_out, root, place) = refs[:7], refs[7:14]
    held, (grad, norm, de, dn, area, mask), arrived = refs[14], refs[15:21], refs[21]
    levels, rows, cols = grad.shape
    arrays = block.shape[0]
    copies = [
        pltpu.make_async_copy(source, target, arrived.at[n])
        for n, (source, target) in enumerate(zip(sources[1:], (grad, norm, de, dn, area, mask)))
    ]
    copies.append(
        pltpu.make_async_copy(sources[0].at[pl.ds(0, held.shape[0])], held, arrived.at[len(copies)])
    )
    for copy in copies:
        copy.start()
    for copy in copies:
        copy.wait()
    block[0:levels] = norm[...] * grad[...]
    block[levels : 2 * levels] = de[...]
    block[2 * levels : 3 * levels] = dn[...]
    block[3 * levels] = mask[...].astype(jnp.float32) / area[...]
    area_out[...] = area[...]
    root[...] = jnp.sqrt(area[...])
    lane = lane_index()
    lat_even = lax.rem(lax.axis_index("lat"), 2) == 0

    def packed(col, first):
        out = {}
        for k, t, row, at in slots(arrays):
            tile = block[k, t * TILE : (t + 1) * TILE, col : col + LANES]
            moved = pltpu.roll(tile, (at - first) % LANES, 1)
            inside = (lane >= at) & (lane < at + ITERS)
            out[row] = jnp.where(inside, moved, out.get(row, jnp.zeros_like(moved)))
        return out

    east, west = packed(cols - LANES, LANES - ITERS), packed(0, 0)
    count = len(east)
    for row in range(count):
        here = slice(row * TILE, (row + 1) * TILE)
        there = slice((count + row) * TILE, (count + row + 1) * TILE)
        edges[here], edges[there] = east[row], west[row]

    sub = lax.broadcasted_iota(jnp.int32, (TILE, LANES), 0)
    for c in range(cols // LANES):
        at = slice(c * LANES, (c + 1) * LANES)
        base = c * (arrays + 2) * TILE
        extra = {}
        for k in range(arrays):
            low, high = block[k, 0:TILE, at], block[k, TILE : 2 * TILE, at]
            here = slice(base + k * TILE, base + (k + 1) * TILE)
            x_rows[here] = jnp.where(lat_even, high, low)
            y_rows[here] = jnp.where(lat_even, low, high)
            lift = 2 * (k % 4)
            inside = (sub >= lift) & (sub < lift + 2)
            north = pltpu.roll(low, (lift + 2) % TILE, 0)
            south = pltpu.roll(high, lift, 0)
            north_held, south_held = extra.get(k // 4, (jnp.zeros_like(low),) * 2)
            extra[k // 4] = (jnp.where(inside, north, north_held), jnp.where(inside, south, south_held))
        for e, (north, south) in extra.items():
            here = slice(base + (arrays + e) * TILE, base + (arrays + e + 1) * TILE)
            x_rows[here] = jnp.where(lat_even, north, south)
            y_rows[here] = jnp.where(lat_even, south, north)
    moved = held[0] + ITERS
    q = lax.rem(lax.div(moved, cols), lax.axis_size("lon"))
    offset = lax.rem(moved, cols) - ITERS
    place[...] = jnp.full((TILE, LANES), jnp.where(lax.broadcasted_iota(jnp.int32, (TILE, LANES), 1) == 0, 2 * q + jnp.where(offset < ITERS - 1, 1, 0), offset))


def join_kernel(edges, mate, to_east, to_west):
    half = edges.shape[0] // 2
    low, high = slice(0, half), slice(half, 2 * half)
    to_east[low], to_west[low] = edges[low], edges[high]
    to_east[high], to_west[high] = mate[low], mate[high]


def after_kernel(count, *refs):
    for source, target in zip(refs[:count], refs[-count:]):
        target[...] = source[...]


def near_kernel(x_rows, y_rows, even_east, even_west, odd_east, odd_west, x_out, y_out):
    rows, tall = x_rows.shape[0], even_east.shape[0]
    half = tall // 2
    lon_even = lax.rem(lax.axis_index("lon"), 2) == 0
    x_out[0:rows] = x_rows[...]
    y_out[0:rows] = y_rows[...]
    east = jnp.where(lon_even, even_east[...], odd_east[...])
    west = jnp.where(lon_even, even_west[...], odd_west[...])
    x_out[rows : rows + tall] = east
    x_out[rows + tall : rows + 2 * tall] = west
    y_out[rows : rows + half] = east[0:half]
    y_out[rows + half : rows + tall] = west[0:half]


def reversed_lanes(x):
    index = LANES - 1 - lane_index(x.shape[0])
    return jnp.take_along_axis(x, index, axis=1, mode="promise_in_bounds")


def fold_kernel(levels, place, f0, f1, f2, out, placed, arrived):
    copy = pltpu.make_async_copy(place, placed, arrived)
    copy.start()
    arrays, rows, wide = out.shape
    cols = wide - LANES
    tiles_across = cols // LANES
    band = (arrays + 2) * TILE
    copy.wait()
    offset = placed[0, 1]
    span = 3 * cols
    far = lane_index(rows)
    for k in range(arrays):
        east_face = levels <= k < 2 * levels
        north_face = 2 * levels <= k < 3 * levels
        pieces = []
        for f in (f0, f1, f2):
            for c in range(tiles_across - 1, -1, -1):
                main = f[c * band + k * TILE : c * band + (k + 1) * TILE]
                few = f[c * band + (arrays + k // 4) * TILE : c * band + (arrays + k // 4 + 1) * TILE]
                few = pltpu.roll(few, (TILE - 2 - 2 * (k % 4)) % TILE, 0)
                pieces.append(reversed_lanes(jnp.concatenate([few, main], axis=0)))
        shift = offset + span - cols + (0 if east_face else 1)
        turned = pltpu.roll(jnp.concatenate(pieces, axis=1), shift, 1)
        beyond = turned[:, cols : cols + LANES]
        before = turned[:, span - LANES :]
        side = jnp.where(far < ITERS, beyond, jnp.where(far >= LANES - ITERS, before, 0.0))
        mirrored = jnp.concatenate([turned[:, :cols], side], axis=1)
        skip = 1 if north_face else 0
        for row in range(rows - 1):
            source = max(rows - 1 - skip - row, 0)
            out[k, row : row + 1] = mirrored[source : source + 1]
        out[k, rows - 1 : rows] = mirrored[rows - 1 : rows]


def steps_kernel(levels, own, x_out, x_in, y_in, area, root, mirrored, out, ext):
    arrays, rows, cols = own.shape
    wide, tall = cols + LANES, 3 * rows
    tiles_across = cols // LANES
    band = (arrays + 2) * TILE
    data = band * tiles_across
    edge = (x_in.shape[0] - data) // 4
    lat = lax.axis_index("lat")
    lat_even = lax.rem(lat, 2) == 0
    at_top = lat == lax.axis_size("lat") - 1
    below_top = lat == lax.axis_size("lat") - 2
    lane = lane_index()

    def put_sides(start, from_east, from_west):
        for k, t, row, at in slots(arrays):
            here = slice(row * TILE, (row + 1) * TILE)
            east = pltpu.roll(from_east[here], (-at) % LANES, 1)
            west = pltpu.roll(from_west[here], (LANES - ITERS - at) % LANES, 1)
            side = jnp.where(lane < ITERS, east, jnp.where(lane >= LANES - ITERS, west, 0.0))
            ext[k, start + t * TILE : start + (t + 1) * TILE, cols:wide] = side

    def put_rows(start, main, spare, lift_base, rows_of):
        for c in range(tiles_across):
            at = slice(c * LANES, (c + 1) * LANES)
            for k in range(arrays):
                base = c * band
                ext[k, start + main * TILE : start + (main + 1) * TILE, at] = rows_of(base + k * TILE)
                few = rows_of(base + (arrays + k // 4) * TILE)
                lift = (lift_base - 2 * (k % 4)) % TILE
                ext[k, start + spare * TILE : start + (spare + 1) * TILE, at] = pltpu.roll(few, lift, 0)

    for k in range(arrays):
        ext[k, rows : 2 * rows, 0:cols] = own[k]
    def part(held, at):
        return held[data + at * edge : data + (at + 1) * edge]

    x_east, x_west = part(x_in, 0), part(x_in, 2)
    y_east, y_west = part(y_in, 0), part(y_in, 1)
    put_sides(
        rows,
        jnp.where(at_top, part(x_in, 1), part(x_out, 0)),
        jnp.where(at_top, part(x_in, 3), part(x_out, 2)),
    )

    def south_rows(at):
        return jnp.where(lat_even, y_in[at : at + TILE], x_in[at : at + TILE])

    def north_rows(at):
        return jnp.where(lat_even, x_in[at : at + TILE], y_in[at : at + TILE])

    put_rows(0, 1, 0, TILE - 2, south_rows)
    put_sides(0, jnp.where(lat_even, y_east, x_east), jnp.where(lat_even, y_west, x_west))

    @pl.when(jnp.logical_not(at_top))
    def _():
        put_rows(2 * rows, 0, 1, 0, north_rows)
        put_sides(
            2 * rows,
            jnp.where(below_top, part(x_out, 1), jnp.where(lat_even, x_east, y_east)),
            jnp.where(below_top, part(x_out, 3), jnp.where(lat_even, x_west, y_west)),
        )

    @pl.when(at_top)
    def _():
        for k in range(arrays):
            ext[k, 2 * rows : 3 * rows] = mirrored[k]
        for k in range(2 * levels, 3 * levels):
            face = ext[k, 2 * rows - 1 : 2 * rows]
            ext[k, 2 * rows - 1 : 2 * rows] = 0.5 * (face + mirrored[k, rows - 1 : rows])

    def east_of(x):
        return pltpu.roll(x, wide - 1, 1)

    def west_of(x):
        return pltpu.roll(x, 1, 1)

    def north_of(x):
        return pltpu.roll(x, x.shape[0] - 1, 0)

    def south_of(x):
        return pltpu.roll(x, 1, 0)

    weight = ext[3 * levels]
    sea = jnp.where(weight > 0.0, 1.0, 0.0)
    sea_east = sea * east_of(sea)
    sea_north = sea * north_of(sea)
    inner = slice(TILE, tall - TILE)
    coefs, values = [], []
    for level in range(levels):
        east = ext[levels + level] * sea_east
        north = ext[2 * levels + level] * sea_north
        west, south = west_of(east), south_of(north)
        rest = 1.0 - weight * ((east + west) + (north + south))
        coefs.append([rest] + [weight * x for x in (east, west, north, south)])
        values.append(weight * ext[level])
    for turn in range(ITERS):
        for level in range(levels):
            u = values[level]
            rest, east, west, north, south = coefs[level]
            u = (rest * u + (east * east_of(u) + west * west_of(u))) + (
                north * north_of(u) + south * south_of(u)
            )
            if turn == 1:
                u = u[inner]
                coefs[level] = [x[inner] for x in coefs[level]]
            values[level] = u
    start = rows - TILE
    own_weight = weight[rows : 2 * rows, :cols]
    for level in range(levels):
        u = values[level][start : start + rows, :cols]
        state = jnp.where(own_weight > 0.0, u * area[...], own[level])
        out[level] = state / root[...]


VMEM = pl.BlockSpec(memory_space=pltpu.VMEM)
SMEM = pl.BlockSpec(memory_space=pltpu.SMEM)
ANY = pl.BlockSpec(memory_space=pl.ANY)
HBM = pl.BlockSpec(memory_space=pltpu.HBM)
PARAMS = pltpu.CompilerParams(vmem_limit_bytes=8 * 1024 * 1024)


def per_device(gradient, norm_factor, diff_east, diff_north, cell_area, sea_mask, partner):
    levels, rows, cols = gradient.shape
    arrays = 3 * levels + 1
    lon_count, lat_count = lax.axis_size("lon"), lax.axis_size("lat")

    def held(*shape):
        return jax.ShapeDtypeStruct(shape, jnp.float32)

    inputs = (gradient, norm_factor, diff_east, diff_north, cell_area, sea_mask)
    edge = (slots(arrays)[-1][2] + 1) * TILE
    data = (arrays + 2) * TILE * (cols // LANES)
    block, edges, x_rows, y_rows, copied_area, root, place = pl.pallas_call(
        pack_kernel,
        out_shape=(
            held(arrays, rows, cols),
            held(2 * edge, LANES),
            held(data, LANES),
            held(data, LANES),
            held(rows, cols),
            held(rows, cols),
            jax.ShapeDtypeStruct((TILE, LANES), jnp.int32),
        ),
        in_specs=[HBM] * 7,
        out_specs=(VMEM,) * 7,
        scratch_shapes=[pltpu.SMEM((LANES,), jnp.int32)]
        + [pltpu.VMEM(x.shape, x.dtype) for x in inputs]
        + [pltpu.SemaphoreType.DMA((7,))],
        compiler_params=PARAMS,
    )(*[pltpu.with_memory_space_constraint(x, pltpu.HBM) for x in (partner, *inputs)])

    def flat(lon, lat):
        return (lon % lon_count) * lat_count + lat

    top = lat_count - 1
    around = range(lon_count)

    def swap(pairs):
        return [pair for a, b in pairs for pair in ((a, b), (b, a))]

    def sent(start, step):
        return [(flat(p, i), flat(p + step, i)) for p in around[start::2] for i in range(top)]

    def lat_swap(start):
        return swap([(flat(p, i), flat(p, i + 1)) for p in around for i in range(start, top, 2)])

    def mirror(total):
        return [(flat(total - p, top), flat(p, top)) for p in around]

    mate = lax.ppermute(edges, AXES, [(flat(p, top), flat(p, top - 1)) for p in around])
    to_east, to_west = pl.pallas_call(
        join_kernel,
        out_shape=(held(2 * edge, LANES),) * 2,
        in_specs=[VMEM] * 2,
        out_specs=(VMEM,) * 2,
        compiler_params=PARAMS,
    )(edges, mate)
    even_east = lax.ppermute(to_west, AXES, sent(1, -1))
    even_west = lax.ppermute(to_east, AXES, sent(1, 1))

    def after(values, first):
        return pl.pallas_call(
            functools.partial(after_kernel, len(values)),
            out_shape=tuple(jax.ShapeDtypeStruct(x.shape, x.dtype) for x in values),
            in_specs=[VMEM] * len(values) + [ANY] * len(first),
            out_specs=(VMEM,) * len(values),
            compiler_params=PARAMS,
        )(*values, *first)

    mirrored_shape = (arrays, rows, cols + LANES)

    def fold(total, third):
        def run(place, x):
            f0 = lax.ppermute(x, AXES, mirror(total))
            f1 = lax.ppermute(x, AXES, mirror(total - 1))
            f2 = lax.ppermute(x, AXES, mirror(total - 2)) if third else x
            return pl.pallas_call(
                functools.partial(fold_kernel, levels),
                out_shape=held(*mirrored_shape),
                in_specs=[ANY] + [VMEM] * 3,
                out_specs=VMEM,
                scratch_shapes=[pltpu.SMEM((TILE, LANES), jnp.int32), pltpu.SemaphoreType.DMA],
                compiler_params=PARAMS,
            )(place, f0, f1, f2)

        return run

    def no_fold(place, x):
        return jnp.zeros(mirrored_shape, jnp.float32)

    (where,) = after((place,), (to_east,))
    chosen = jnp.where(lax.axis_index("lat") == top, where[0, 0] + 1, 0)
    folds = [fold(total, third) for total in around for third in (False, True)]
    mirrored = lax.switch(chosen, [no_fold] + folds, where, y_rows)
    go_east, go_west = after((to_east, to_west), (even_east, even_west, mirrored))
    odd_west = lax.ppermute(go_east, AXES, sent(0, 1))
    odd_east = lax.ppermute(go_west, AXES, sent(0, -1))
    x_out, y_out = pl.pallas_call(
        near_kernel,
        out_shape=(held(data + 4 * edge, LANES), held(data + 2 * edge, LANES)),
        in_specs=[VMEM] * 6,
        out_specs=(VMEM, VMEM),
        compiler_params=PARAMS,
    )(x_rows, y_rows, even_east, even_west, odd_east, odd_west)
    x_in = lax.ppermute(x_out, AXES, lat_swap(0))
    y_in = lax.ppermute(y_out, AXES, lat_swap(1))
    return pl.pallas_call(
        functools.partial(steps_kernel, levels),
        out_shape=held(levels, rows, cols),
        in_specs=[VMEM] * 7,
        out_specs=VMEM,
        scratch_shapes=[pltpu.VMEM((arrays, 3 * rows, cols + LANES), jnp.float32)],
        compiler_params=PARAMS,
    )(block, x_out, x_in, y_in, copied_area, root, mirrored)


def solution(mesh):
    return jax.shard_map(
        per_device,
        mesh=mesh,
        in_specs=(
            P(None, "lat", "lon"),
            P(None, "lat", "lon"),
            P(None, "lat", "lon"),
            P(None, "lat", "lon"),
            P("lat", "lon"),
            P("lat", "lon"),
            P(),
        ),
        out_specs=P(None, "lat", "lon"),
        check_vma=False,
    )
```

```python
import functools

import jax
import jax.numpy as jnp
from jax import lax
from jax.experimental import pallas as pl
from jax.experimental.pallas import tpu as pltpu
from jax.sharding import PartitionSpec as P

ITERS = 10
LANES = 128
TILE = 8
PER_ROW = LANES // ITERS
AXES = ("lon", "lat")


def lane_index(rows=TILE):
    return lax.broadcasted_iota(jnp.int32, (rows, LANES), 1)


def slots(arrays):
    places = [(k, t) for k in range(arrays) for t in range(2)]
    return [(k, t, m // PER_ROW, (m % PER_ROW) * ITERS) for m, (k, t) in enumerate(places)]


def pack_kernel(*refs):
    sources, (block, edges, x_rows, y_rows, area_out, root, place, chosen) = refs[:7], refs[7:15]
    held, (grad, norm, de, dn, area, mask), arrived = refs[15], refs[16:22], refs[22]
    levels, rows, cols = grad.shape
    arrays = block.shape[0]
    copies = [
        pltpu.make_async_copy(source, target, arrived.at[n])
        for n, (source, target) in enumerate(zip(sources[1:], (grad, norm, de, dn, area, mask)))
    ]
    copies.append(
        pltpu.make_async_copy(sources[0].at[pl.ds(0, held.shape[0])], held, arrived.at[len(copies)])
    )
    for copy in copies:
        copy.start()
    for copy in copies:
        copy.wait()
    block[0:levels] = norm[...] * grad[...]
    block[levels : 2 * levels] = de[...]
    block[2 * levels : 3 * levels] = dn[...]
    block[3 * levels] = mask[...].astype(jnp.float32) / area[...]
    area_out[...] = area[...]
    root[...] = jnp.sqrt(area[...])
    lane = lane_index()
    lat_even = lax.rem(lax.axis_index("lat"), 2) == 0

    def packed(col, first):
        out = {}
        for k, t, row, at in slots(arrays):
            tile = block[k, t * TILE : (t + 1) * TILE, col : col + LANES]
            moved = pltpu.roll(tile, (at - first) % LANES, 1)
            inside = (lane >= at) & (lane < at + ITERS)
            out[row] = jnp.where(inside, moved, out.get(row, jnp.zeros_like(moved)))
        return out

    east, west = packed(cols - LANES, LANES - ITERS), packed(0, 0)
    count = len(east)
    for row in range(count):
        here = slice(row * TILE, (row + 1) * TILE)
        there = slice((count + row) * TILE, (count + row + 1) * TILE)
        edges[here], edges[there] = east[row], west[row]

    sub = lax.broadcasted_iota(jnp.int32, (TILE, LANES), 0)
    for c in range(cols // LANES):
        at = slice(c * LANES, (c + 1) * LANES)
        base = c * (arrays + 2) * TILE
        extra = {}
        for k in range(arrays):
            low, high = block[k, 0:TILE, at], block[k, TILE : 2 * TILE, at]
            here = slice(base + k * TILE, base + (k + 1) * TILE)
            x_rows[here] = jnp.where(lat_even, high, low)
            y_rows[here] = jnp.where(lat_even, low, high)
            lift = 2 * (k % 4)
            inside = (sub >= lift) & (sub < lift + 2)
            north = pltpu.roll(low, (lift + 2) % TILE, 0)
            south = pltpu.roll(high, lift, 0)
            north_held, south_held = extra.get(k // 4, (jnp.zeros_like(low),) * 2)
            extra[k // 4] = (jnp.where(inside, north, north_held), jnp.where(inside, south, south_held))
        for e, (north, south) in extra.items():
            here = slice(base + (arrays + e) * TILE, base + (arrays + e + 1) * TILE)
            x_rows[here] = jnp.where(lat_even, north, south)
            y_rows[here] = jnp.where(lat_even, south, north)
    moved = held[0] + ITERS
    q = lax.rem(lax.div(moved, cols), lax.axis_size("lon"))
    offset = lax.rem(moved, cols) - ITERS
    place[...] = jnp.full((TILE, LANES), offset)
    at_top = lax.axis_index("lat") == lax.axis_size("lat") - 1
    chosen[...] = jnp.full((1,), jnp.where(at_top, 1 + 2 * q + jnp.where(offset < ITERS - 1, 1, 0), 0))


def join_kernel(edges, mate, to_east, to_west):
    half = edges.shape[0] // 2
    low, high = slice(0, half), slice(half, 2 * half)
    to_east[low], to_west[low] = edges[low], edges[high]
    to_east[high], to_west[high] = mate[low], mate[high]


def after_kernel(count, *refs):
    for source, target in zip(refs[:count], refs[-count:]):
        target[...] = source[...]


def after(values, *first):
    values = values if isinstance(values, tuple) else (values,)
    handed = pl.pallas_call(
        functools.partial(after_kernel, len(values)),
        out_shape=tuple(jax.ShapeDtypeStruct(x.shape, x.dtype) for x in values),
        in_specs=[VMEM] * len(values) + [ANY] * len(first),
        out_specs=(VMEM,) * len(values),
        compiler_params=PARAMS,
    )(*values, *first)
    return handed if len(values) > 1 else handed[0]


def near_kernel(x_rows, y_rows, east, west, x_out, y_out):
    rows, tall = x_rows.shape[0], east.shape[0]
    half = tall // 2
    x_out[0:rows] = x_rows[...]
    y_out[0:rows] = y_rows[...]
    x_out[rows : rows + tall] = east[...]
    x_out[rows + tall : rows + 2 * tall] = west[...]
    y_out[rows : rows + half] = east[0:half]
    y_out[rows + half : rows + tall] = west[0:half]
    y_out[rows + tall : y_out.shape[0]] = jnp.zeros((y_out.shape[0] - rows - tall, LANES), jnp.float32)


def reversed_lanes(x):
    index = LANES - 1 - lane_index(x.shape[0])
    return jnp.take_along_axis(x, index, axis=1, mode="promise_in_bounds")


def fold_kernel(levels, order, place, behind, first, second, third, out, placed, arrived):
    del behind
    blocks = dict(zip(order, (first, second, third)))
    copy = pltpu.make_async_copy(place, placed, arrived)
    copy.start()
    arrays, rows, wide = out.shape
    cols = wide - LANES
    tiles_across = cols // LANES
    band = (arrays + 2) * TILE
    copy.wait()
    offset = placed[0, 0]
    span = 3 * cols
    far = lane_index(rows)

    for k in range(arrays):
        east_face = levels <= k < 2 * levels
        north_face = 2 * levels <= k < 3 * levels
        pieces = []
        for f in (blocks[n] for n in range(3)):
            for c in range(tiles_across - 1, -1, -1):
                main_at = c * band + k * TILE
                few_at = c * band + (arrays + k // 4) * TILE
                main, few = f[main_at : main_at + TILE], f[few_at : few_at + TILE]
                few = pltpu.roll(few, (TILE - 2 - 2 * (k % 4)) % TILE, 0)
                pieces.append(reversed_lanes(jnp.concatenate([few, main], axis=0)))
        shift = offset + span - cols + (0 if east_face else 1)
        turned = pltpu.roll(jnp.concatenate(pieces, axis=1), shift, 1)
        beyond = turned[:, cols : cols + LANES]
        before = turned[:, span - LANES :]
        side = jnp.where(far < ITERS, beyond, jnp.where(far >= LANES - ITERS, before, 0.0))
        mirrored = jnp.concatenate([turned[:, :cols], side], axis=1)
        skip = 1 if north_face else 0
        for row in range(rows - 1):
            source = max(rows - 1 - skip - row, 0)
            out[k, row : row + 1] = mirrored[source : source + 1]
        out[k, rows - 1 : rows] = mirrored[rows - 1 : rows]


def steps_kernel(levels, own, x_out, x_in, y_in, area, root, mirrored, out, ext):
    arrays, rows, cols = own.shape
    wide, tall = cols + LANES, 3 * rows
    tiles_across = cols // LANES
    band = (arrays + 2) * TILE
    data = band * tiles_across
    edge = (x_in.shape[0] - data) // 4
    lat = lax.axis_index("lat")
    lat_even = lax.rem(lat, 2) == 0
    at_top = lat == lax.axis_size("lat") - 1
    below_top = lat == lax.axis_size("lat") - 2
    lane = lane_index()

    def put_sides(start, from_east, from_west):
        for k, t, row, at in slots(arrays):
            here = slice(row * TILE, (row + 1) * TILE)
            east = pltpu.roll(from_east[here], (-at) % LANES, 1)
            west = pltpu.roll(from_west[here], (LANES - ITERS - at) % LANES, 1)
            side = jnp.where(lane < ITERS, east, jnp.where(lane >= LANES - ITERS, west, 0.0))
            ext[k, start + t * TILE : start + (t + 1) * TILE, cols:wide] = side

    def put_rows(start, main, spare, lift_base, rows_of):
        for c in range(tiles_across):
            at = slice(c * LANES, (c + 1) * LANES)
            for k in range(arrays):
                base = c * band
                ext[k, start + main * TILE : start + (main + 1) * TILE, at] = rows_of(base + k * TILE)
                few = rows_of(base + (arrays + k // 4) * TILE)
                lift = (lift_base - 2 * (k % 4)) % TILE
                ext[k, start + spare * TILE : start + (spare + 1) * TILE, at] = pltpu.roll(few, lift, 0)

    for k in range(arrays):
        ext[k, rows : 2 * rows, 0:cols] = own[k]
    def part(held, at):
        return held[data + at * edge : data + (at + 1) * edge]

    x_east, x_west = part(x_in, 0), part(x_in, 2)
    y_east, y_west = part(y_in, 0), part(y_in, 1)
    put_sides(
        rows,
        jnp.where(at_top, part(x_in, 1), part(x_out, 0)),
        jnp.where(at_top, part(x_in, 3), part(x_out, 2)),
    )

    def south_rows(at):
        return jnp.where(lat_even, y_in[at : at + TILE], x_in[at : at + TILE])

    def north_rows(at):
        return jnp.where(lat_even, x_in[at : at + TILE], y_in[at : at + TILE])

    put_rows(0, 1, 0, TILE - 2, south_rows)
    put_sides(0, jnp.where(lat_even, y_east, x_east), jnp.where(lat_even, y_west, x_west))

    @pl.when(jnp.logical_not(at_top))
    def _():
        put_rows(2 * rows, 0, 1, 0, north_rows)
        put_sides(
            2 * rows,
            jnp.where(below_top, part(x_out, 1), jnp.where(lat_even, x_east, y_east)),
            jnp.where(below_top, part(x_out, 3), jnp.where(lat_even, x_west, y_west)),
        )

    @pl.when(at_top)
    def _():
        for k in range(arrays):
            ext[k, 2 * rows : 3 * rows] = mirrored[k]
        for k in range(2 * levels, 3 * levels):
            face = ext[k, 2 * rows - 1 : 2 * rows]
            ext[k, 2 * rows - 1 : 2 * rows] = 0.5 * (face + mirrored[k, rows - 1 : rows])

    def east_of(x):
        return pltpu.roll(x, wide - 1, 1)

    def west_of(x):
        return pltpu.roll(x, 1, 1)

    def north_of(x):
        return pltpu.roll(x, x.shape[0] - 1, 0)

    def south_of(x):
        return pltpu.roll(x, 1, 0)

    weight = ext[3 * levels]
    sea = jnp.where(weight > 0.0, 1.0, 0.0)
    sea_east = sea * east_of(sea)
    sea_north = sea * north_of(sea)
    inner = slice(TILE, tall - TILE)
    coefs, values = [], []
    for level in range(levels):
        east = ext[levels + level] * sea_east
        north = ext[2 * levels + level] * sea_north
        west, south = west_of(east), south_of(north)
        rest = 1.0 - weight * ((east + west) + (north + south))
        coefs.append([rest] + [weight * x for x in (east, west, north, south)])
        values.append(weight * ext[level])
    for turn in range(ITERS):
        for level in range(levels):
            u = values[level]
            rest, east, west, north, south = coefs[level]
            u = (rest * u + (east * east_of(u) + west * west_of(u))) + (
                north * north_of(u) + south * south_of(u)
            )
            if turn == 1:
                u = u[inner]
                coefs[level] = [x[inner] for x in coefs[level]]
            values[level] = u
    start = rows - TILE
    own_weight = weight[rows : 2 * rows, :cols]
    for level in range(levels):
        u = values[level][start : start + rows, :cols]
        state = jnp.where(own_weight > 0.0, u * area[...], own[level])
        out[level] = state / root[...]


VMEM = pl.BlockSpec(memory_space=pltpu.VMEM)
SMEM = pl.BlockSpec(memory_space=pltpu.SMEM)
ANY = pl.BlockSpec(memory_space=pl.ANY)
HBM = pl.BlockSpec(memory_space=pltpu.HBM)
PARAMS = pltpu.CompilerParams(vmem_limit_bytes=8 * 1024 * 1024)


def per_device(gradient, norm_factor, diff_east, diff_north, cell_area, sea_mask, partner):
    levels, rows, cols = gradient.shape
    arrays = 3 * levels + 1
    lon_count, lat_count = lax.axis_size("lon"), lax.axis_size("lat")

    def held(*shape):
        return jax.ShapeDtypeStruct(shape, jnp.float32)

    inputs = (gradient, norm_factor, diff_east, diff_north, cell_area, sea_mask)
    edge = (slots(arrays)[-1][2] + 1) * TILE
    data = (arrays + 2) * TILE * (cols // LANES)
    block, edges, x_rows, y_rows, copied_area, root, place, chosen = pl.pallas_call(
        pack_kernel,
        out_shape=(
            held(arrays, rows, cols),
            held(2 * edge, LANES),
            held(data, LANES),
            held(data, LANES),
            held(rows, cols),
            held(rows, cols),
            jax.ShapeDtypeStruct((TILE, LANES), jnp.int32),
            jax.ShapeDtypeStruct((1,), jnp.int32),
        ),
        in_specs=[HBM] * 7,
        out_specs=(VMEM,) * 8,
        scratch_shapes=[pltpu.SMEM((LANES,), jnp.int32)]
        + [pltpu.VMEM(x.shape, x.dtype) for x in inputs]
        + [pltpu.SemaphoreType.DMA((7,))],
        compiler_params=PARAMS,
    )(*[pltpu.with_memory_space_constraint(x, pltpu.HBM) for x in (partner, *inputs)])

    def flat(lon, lat):
        return (lon % lon_count) * lat_count + lat

    top = lat_count - 1
    around = range(lon_count)

    def swap(pairs):
        return [pair for a, b in pairs for pair in ((a, b), (b, a))]

    def sent(start, step):
        return [(flat(p, i), flat(p + step, i)) for p in around[start::2] for i in range(top)]

    def lat_swap(start, parity):
        return swap(
            [(flat(p, i), flat(p, i + 1)) for p in around[parity::2] for i in range(start, top, 2)]
        )

    def mirror(total):
        return [(flat(total - p, top), flat(p, top)) for p in around]

    mate = lax.ppermute(edges, AXES, [(flat(p, top), flat(p, top - 1)) for p in around])
    to_east, to_west = pl.pallas_call(
        join_kernel,
        out_shape=(held(2 * edge, LANES),) * 2,
        in_specs=[VMEM] * 2,
        out_specs=(VMEM,) * 2,
        compiler_params=PARAMS,
    )(edges, mate)
    even_east = lax.ppermute(to_west, AXES, sent(1, -1))
    even_west = lax.ppermute(to_east, AXES, sent(1, 1))

    mirrored_shape = (arrays, rows, cols + LANES)

    def fold(total, third):
        totals = [total, total - 1] + [total - 2] * third
        order = sorted(range(3), key=lambda n: totals[n] % 2 if n < len(totals) else -1)

        def run(x, place, behind):
            blocks = [lax.ppermute(x, AXES, mirror(t)) for t in totals] + [x] * (3 - len(totals))
            return pl.pallas_call(
                functools.partial(fold_kernel, levels, order),
                out_shape=held(*mirrored_shape),
                in_specs=[ANY] * 2 + [VMEM] * 3,
                out_specs=VMEM,
                scratch_shapes=[pltpu.SMEM((TILE, LANES), jnp.int32), pltpu.SemaphoreType.DMA],
                compiler_params=PARAMS,
            )(place, behind, *(blocks[n] for n in order))

        return run

    def no_fold(x, place, behind):
        return jnp.zeros(mirrored_shape, jnp.float32)

    folds = [fold(total, third) for total in around for third in (False, True)]
    mirrored = lax.switch(chosen[0], [no_fold] + folds, y_rows, place, to_east)

    def near(east, west):
        return pl.pallas_call(
            near_kernel,
            out_shape=(held(data + 4 * edge, LANES), held(data + 4 * edge + TILE, LANES)),
            in_specs=[VMEM] * 4,
            out_specs=(VMEM,) * 2,
            compiler_params=PARAMS,
        )(x_rows, y_rows, east, west)

    def steps(x_out, x_in, y_in):
        return pl.pallas_call(
            functools.partial(steps_kernel, levels),
            out_shape=held(levels, rows, cols),
            in_specs=[VMEM] * 7,
            out_specs=VMEM,
            scratch_shapes=[pltpu.VMEM((arrays, 3 * rows, cols + LANES), jnp.float32)],
            compiler_params=PARAMS,
        )(block, x_out, x_in, y_in, copied_area, root, mirrored)

    x_out, y_out = near(even_east, even_west)
    go_east, go_west = after((to_east, to_west), y_out, mirrored)
    y_in = lax.ppermute(y_out, AXES, lat_swap(1, 0))
    odd_west = lax.ppermute(go_east, AXES, sent(0, 1))
    odd_east = lax.ppermute(go_west, AXES, sent(0, -1))
    x_in = lax.ppermute(after(x_out, odd_west, odd_east), AXES, lat_swap(0, 0))

    def even_steps(x_out, x_in, y_in, east, west):
        return steps(x_out, x_in, y_in)

    def odd_steps(x_out, x_in, y_in, east, west):
        x_out, y_out = near(east, west)
        y_in = lax.ppermute(y_out, AXES, lat_swap(1, 1))
        x_in = lax.ppermute(x_out, AXES, lat_swap(0, 1))
        return steps(x_out, x_in, y_in)

    return lax.switch(
        lax.rem(lax.axis_index("lon"), 2),
        [even_steps, odd_steps],
        x_out,
        x_in,
        y_in,
        odd_east,
        odd_west,
    )


def solution(mesh):
    return jax.shard_map(
        per_device,
        mesh=mesh,
        in_specs=(
            P(None, "lat", "lon"),
            P(None, "lat", "lon"),
            P(None, "lat", "lon"),
            P(None, "lat", "lon"),
            P("lat", "lon"),
            P("lat", "lon"),
            P(),
        ),
        out_specs=P(None, "lat", "lon"),
        check_vma=False,
    )
```

```python
import functools

import jax
import jax.numpy as jnp
from jax import lax
from jax.experimental import pallas as pl
from jax.experimental.pallas import tpu as pltpu
from jax.sharding import PartitionSpec as P

ITERS = 10
LANES = 128
TILE = 8
PER_ROW = LANES // ITERS
AXES = ("lon", "lat")


def lane_index(rows=TILE):
    return lax.broadcasted_iota(jnp.int32, (rows, LANES), 1)


def slots(arrays):
    places = [(k, t) for k in range(arrays) for t in range(2)]
    return [(k, t, m // PER_ROW, (m % PER_ROW) * ITERS) for m, (k, t) in enumerate(places)]


def early():
    at_top = lax.axis_index("lat") == lax.axis_size("lat") - 1
    return (lax.rem(lax.axis_index("lon"), 2) == 1) | at_top


def pack_kernel(*refs):
    (partner, *sources), outs, place = refs[:7], refs[7:13], refs[13]
    targets, held, arrived = refs[14:20], refs[20], refs[21]
    cols = targets[0].shape[2]

    @pl.when(early())
    def _():
        extra = pltpu.make_async_copy(partner.at[pl.ds(0, held.shape[0])], held, arrived.at[6])
        extra.start()
        pack(sources, targets, arrived, *outs)
        extra.wait()
        moved = held[0] + ITERS
        q = lax.rem(lax.div(moved, cols), lax.axis_size("lon"))
        offset = lax.rem(moved, cols) - ITERS
        branch = 2 * q + jnp.where(offset < ITERS - 1, 1, 0)
        place[...] = jnp.where(lane_index() == 0, branch, offset)


def late_pack_kernel(*refs):
    sources, firsts, outs = refs[:6], refs[6:12], refs[13:19]
    targets, arrived = refs[19:25], refs[25]

    @pl.when(jnp.logical_not(early()))
    def _():
        pack(sources, targets, arrived, *outs)

    @pl.when(early() & (lax.rem(lax.axis_index("lon"), 2) == 0))
    def _():
        for first, out in zip(firsts, outs):
            out[...] = first[...]


def pack(sources, targets, arrived, block, edges, x_rows, y_rows, area_out, root):
    grad, norm, de, dn, area, mask = targets
    levels, rows, cols = grad.shape
    arrays = block.shape[0]
    copies = [
        pltpu.make_async_copy(source, target, arrived.at[n])
        for n, (source, target) in enumerate(zip(sources, targets))
    ]
    for copy in copies:
        copy.start()
    for copy in copies:
        copy.wait()
    block[0:levels] = norm[...] * grad[...]
    block[levels : 2 * levels] = de[...]
    block[2 * levels : 3 * levels] = dn[...]
    block[3 * levels] = mask[...].astype(jnp.float32) / area[...]
    area_out[...] = area[...]
    root[...] = jnp.sqrt(area[...])
    lane = lane_index()
    lat_even = lax.rem(lax.axis_index("lat"), 2) == 0

    def packed(col, first):
        out = {}
        for k, t, row, at in slots(arrays):
            tile = block[k, t * TILE : (t + 1) * TILE, col : col + LANES]
            moved = pltpu.roll(tile, (at - first) % LANES, 1)
            inside = (lane >= at) & (lane < at + ITERS)
            out[row] = jnp.where(inside, moved, out.get(row, jnp.zeros_like(moved)))
        return out

    east, west = packed(cols - LANES, LANES - ITERS), packed(0, 0)
    count = len(east)
    for row in range(count):
        here = slice(row * TILE, (row + 1) * TILE)
        there = slice((count + row) * TILE, (count + row + 1) * TILE)
        edges[here], edges[there] = east[row], west[row]

    sub = lax.broadcasted_iota(jnp.int32, (TILE, LANES), 0)
    for c in range(cols // LANES):
        at = slice(c * LANES, (c + 1) * LANES)
        base = c * (arrays + 2) * TILE
        extra = {}
        for k in range(arrays):
            low, high = block[k, 0:TILE, at], block[k, TILE : 2 * TILE, at]
            here = slice(base + k * TILE, base + (k + 1) * TILE)
            x_rows[here] = jnp.where(lat_even, high, low)
            y_rows[here] = jnp.where(lat_even, low, high)
            lift = 2 * (k % 4)
            inside = (sub >= lift) & (sub < lift + 2)
            north = pltpu.roll(low, (lift + 2) % TILE, 0)
            south = pltpu.roll(high, lift, 0)
            north_held, south_held = extra.get(k // 4, (jnp.zeros_like(low),) * 2)
            extra[k // 4] = (jnp.where(inside, north, north_held), jnp.where(inside, south, south_held))
        for e, (north, south) in extra.items():
            here = slice(base + (arrays + e) * TILE, base + (arrays + e + 1) * TILE)
            x_rows[here] = jnp.where(lat_even, north, south)
            y_rows[here] = jnp.where(lat_even, south, north)


def join_kernel(edges, mate, to_east, to_west):
    half = edges.shape[0] // 2
    low, high = slice(0, half), slice(half, 2 * half)
    to_east[low], to_west[low] = edges[low], edges[high]
    to_east[high], to_west[high] = mate[low], mate[high]


def after_kernel(count, *refs):
    for source, target in zip(refs[:count], refs[-count:]):
        target[...] = source[...]


def after(values, *first):
    values = values if isinstance(values, tuple) else (values,)
    handed = pl.pallas_call(
        functools.partial(after_kernel, len(values)),
        out_shape=tuple(jax.ShapeDtypeStruct(x.shape, x.dtype) for x in values),
        in_specs=[VMEM] * len(values) + [ANY] * len(first),
        out_specs=(VMEM,) * len(values),
        compiler_params=PARAMS,
    )(*values, *first)
    return handed if len(values) > 1 else handed[0]


def near_kernel(x_rows, y_rows, east, west, x_out, y_out):
    rows, tall = x_rows.shape[0], east.shape[0]
    half = tall // 2
    x_out[0:rows] = x_rows[...]
    y_out[0:rows] = y_rows[...]
    x_out[rows : rows + tall] = east[...]
    x_out[rows + tall : rows + 2 * tall] = west[...]
    y_out[rows : rows + half] = east[0:half]
    y_out[rows + half : rows + tall] = west[0:half]
    y_out[rows + tall : y_out.shape[0]] = jnp.zeros((y_out.shape[0] - rows - tall, LANES), jnp.float32)


def reversed_lanes(x):
    index = LANES - 1 - lane_index(x.shape[0])
    return jnp.take_along_axis(x, index, axis=1, mode="promise_in_bounds")


def fold_kernel(levels, used, place, *refs):
    blocks, (out, placed, arrived) = refs[:-3], refs[-3:]
    lon_even = lax.rem(lax.axis_index("lon"), 2) == 0
    copy = pltpu.make_async_copy(place, placed, arrived)
    copy.start()
    arrays, rows, wide = out.shape
    cols = wide - LANES
    tiles_across = cols // LANES
    band = (arrays + 2) * TILE
    copy.wait()
    offset = placed[0, 1]
    span = 3 * cols
    far = lane_index(rows)

    for k in range(arrays):
        east_face = levels <= k < 2 * levels
        north_face = 2 * levels <= k < 3 * levels
        pieces = []
        for even, odd in used:
            for c in range(tiles_across - 1, -1, -1):
                main_at = c * band + k * TILE
                few_at = c * band + (arrays + k // 4) * TILE
                main, few = (
                    jnp.where(lon_even, blocks[even][at : at + TILE], blocks[odd][at : at + TILE])
                    for at in (main_at, few_at)
                )
                few = pltpu.roll(few, (TILE - 2 - 2 * (k % 4)) % TILE, 0)
                pieces.append(reversed_lanes(jnp.concatenate([few, main], axis=0)))
        shift = offset + span - cols + (0 if east_face else 1)
        turned = pltpu.roll(jnp.concatenate(pieces, axis=1), shift, 1)
        beyond = turned[:, cols : cols + LANES]
        before = turned[:, span - LANES :]
        side = jnp.where(far < ITERS, beyond, jnp.where(far >= LANES - ITERS, before, 0.0))
        mirrored = jnp.concatenate([turned[:, :cols], side], axis=1)
        skip = 1 if north_face else 0
        for row in range(rows - 1):
            source = max(rows - 1 - skip - row, 0)
            out[k, row : row + 1] = mirrored[source : source + 1]
        out[k, rows - 1 : rows] = mirrored[rows - 1 : rows]


def steps_kernel(levels, own, x_out, x_in, y_in, area, root, mirrored, out, ext):
    arrays, rows, cols = own.shape
    wide, tall = cols + LANES, 3 * rows
    tiles_across = cols // LANES
    band = (arrays + 2) * TILE
    data = band * tiles_across
    edge = (x_in.shape[0] - data) // 4
    lat = lax.axis_index("lat")
    lat_even = lax.rem(lat, 2) == 0
    at_top = lat == lax.axis_size("lat") - 1
    below_top = lat == lax.axis_size("lat") - 2
    lane = lane_index()

    def put_sides(start, from_east, from_west):
        for k, t, row, at in slots(arrays):
            here = slice(row * TILE, (row + 1) * TILE)
            east = pltpu.roll(from_east[here], (-at) % LANES, 1)
            west = pltpu.roll(from_west[here], (LANES - ITERS - at) % LANES, 1)
            side = jnp.where(lane < ITERS, east, jnp.where(lane >= LANES - ITERS, west, 0.0))
            ext[k, start + t * TILE : start + (t + 1) * TILE, cols:wide] = side

    def put_rows(start, main, spare, lift_base, rows_of):
        for c in range(tiles_across):
            at = slice(c * LANES, (c + 1) * LANES)
            for k in range(arrays):
                base = c * band
                ext[k, start + main * TILE : start + (main + 1) * TILE, at] = rows_of(base + k * TILE)
                few = rows_of(base + (arrays + k // 4) * TILE)
                lift = (lift_base - 2 * (k % 4)) % TILE
                ext[k, start + spare * TILE : start + (spare + 1) * TILE, at] = pltpu.roll(few, lift, 0)

    for k in range(arrays):
        ext[k, rows : 2 * rows, 0:cols] = own[k]
    def part(held, at):
        return held[data + at * edge : data + (at + 1) * edge]

    x_east, x_west = part(x_in, 0), part(x_in, 2)
    y_east, y_west = part(y_in, 0), part(y_in, 1)
    put_sides(
        rows,
        jnp.where(at_top, part(x_in, 1), part(x_out, 0)),
        jnp.where(at_top, part(x_in, 3), part(x_out, 2)),
    )

    def south_rows(at):
        return jnp.where(lat_even, y_in[at : at + TILE], x_in[at : at + TILE])

    def north_rows(at):
        return jnp.where(lat_even, x_in[at : at + TILE], y_in[at : at + TILE])

    put_rows(0, 1, 0, TILE - 2, south_rows)
    put_sides(0, jnp.where(lat_even, y_east, x_east), jnp.where(lat_even, y_west, x_west))

    @pl.when(jnp.logical_not(at_top))
    def _():
        put_rows(2 * rows, 0, 1, 0, north_rows)
        put_sides(
            2 * rows,
            jnp.where(below_top, part(x_out, 1), jnp.where(lat_even, x_east, y_east)),
            jnp.where(below_top, part(x_out, 3), jnp.where(lat_even, x_west, y_west)),
        )

    @pl.when(at_top)
    def _():
        for k in range(arrays):
            ext[k, 2 * rows : 3 * rows] = mirrored[k]
        for k in range(2 * levels, 3 * levels):
            face = ext[k, 2 * rows - 1 : 2 * rows]
            ext[k, 2 * rows - 1 : 2 * rows] = 0.5 * (face + mirrored[k, rows - 1 : rows])

    def east_of(x):
        return pltpu.roll(x, wide - 1, 1)

    def west_of(x):
        return pltpu.roll(x, 1, 1)

    def north_of(x):
        return pltpu.roll(x, x.shape[0] - 1, 0)

    def south_of(x):
        return pltpu.roll(x, 1, 0)

    weight = ext[3 * levels]
    sea = jnp.where(weight > 0.0, 1.0, 0.0)
    sea_east = sea * east_of(sea)
    sea_north = sea * north_of(sea)
    inner = slice(TILE, tall - TILE)
    coefs, values = [], []
    for level in range(levels):
        east = ext[levels + level] * sea_east
        north = ext[2 * levels + level] * sea_north
        west, south = west_of(east), south_of(north)
        rest = 1.0 - weight * ((east + west) + (north + south))
        coefs.append([rest] + [weight * x for x in (east, west, north, south)])
        values.append(weight * ext[level])
    for turn in range(ITERS):
        for level in range(levels):
            u = values[level]
            rest, east, west, north, south = coefs[level]
            u = (rest * u + (east * east_of(u) + west * west_of(u))) + (
                north * north_of(u) + south * south_of(u)
            )
            if turn == 1:
                u = u[inner]
                coefs[level] = [x[inner] for x in coefs[level]]
            values[level] = u
    start = rows - TILE
    own_weight = weight[rows : 2 * rows, :cols]
    for level in range(levels):
        u = values[level][start : start + rows, :cols]
        state = jnp.where(own_weight > 0.0, u * area[...], own[level])
        out[level] = state / root[...]


VMEM = pl.BlockSpec(memory_space=pltpu.VMEM)
SMEM = pl.BlockSpec(memory_space=pltpu.SMEM)
ANY = pl.BlockSpec(memory_space=pl.ANY)
HBM = pl.BlockSpec(memory_space=pltpu.HBM)
PARAMS = pltpu.CompilerParams(vmem_limit_bytes=8 * 1024 * 1024)


def per_device(gradient, norm_factor, diff_east, diff_north, cell_area, sea_mask, partner):
    levels, rows, cols = gradient.shape
    arrays = 3 * levels + 1
    lon_count, lat_count = lax.axis_size("lon"), lax.axis_size("lat")

    def held(*shape):
        return jax.ShapeDtypeStruct(shape, jnp.float32)

    inputs = (gradient, norm_factor, diff_east, diff_north, cell_area, sea_mask)
    edge = (slots(arrays)[-1][2] + 1) * TILE
    data = (arrays + 2) * TILE * (cols // LANES)
    def flat(lon, lat):
        return (lon % lon_count) * lat_count + lat

    top = lat_count - 1
    around = range(lon_count)

    def swap(pairs):
        return [pair for a, b in pairs for pair in ((a, b), (b, a))]

    def sent(start, step):
        return [(flat(p, i), flat(p + step, i)) for p in around[start::2] for i in range(top)]

    def lat_swap(start, parity):
        return swap(
            [(flat(p, i), flat(p, i + 1)) for p in around[parity::2] for i in range(start, top, 2)]
        )

    def mirror(total):
        return [(flat(total - p, top), flat(p, top)) for p in around]

    packed_shapes = (
        held(arrays, rows, cols),
        held(2 * edge, LANES),
        held(data, LANES),
        held(data, LANES),
        held(rows, cols),
        held(rows, cols),
    )
    joined_shapes = (held(2 * edge, LANES),) * 2
    odd = lax.rem(lax.axis_index("lon"), 2)

    def join(edges, mate):
        return pl.pallas_call(
            join_kernel,
            out_shape=joined_shapes,
            in_specs=[VMEM] * 2,
            out_specs=(VMEM,) * 2,
            compiler_params=PARAMS,
        )(edges, mate)

    def in_hbm(*arrays):
        return [pltpu.with_memory_space_constraint(x, pltpu.HBM) for x in arrays]

    buffers = [pltpu.VMEM(x.shape, x.dtype) for x in inputs]
    *early_held, place = pl.pallas_call(
        pack_kernel,
        out_shape=packed_shapes + (jax.ShapeDtypeStruct((TILE, LANES), jnp.int32),),
        in_specs=[HBM] * 7,
        out_specs=(VMEM,) * 7,
        scratch_shapes=buffers
        + [pltpu.SMEM((LANES,), jnp.int32), pltpu.SemaphoreType.DMA((7,))],
        compiler_params=PARAMS,
    )(*in_hbm(partner, *inputs))

    def mates(parity):
        return [(flat(p, top), flat(p, top - 1)) for p in around[parity::2]]

    def fetch(edges):
        return join(edges, lax.ppermute(edges, AXES, mates(1)))

    def no_fetch(edges):
        return join(edges, edges)

    near_top = lax.axis_index("lat") >= top - 1
    edges = early_held[1]
    to_east, to_west = lax.switch(
        (near_top & (odd == 1)).astype(jnp.int32), [no_fetch, fetch], edges
    )
    even_east = lax.ppermute(to_west, AXES, sent(1, -1))
    even_west = lax.ppermute(to_east, AXES, sent(1, 1))

    def late_fetch(edges):
        return after(lax.ppermute(edges, AXES, mates(0)))

    late_mate = lax.switch(
        (near_top & (odd == 0)).astype(jnp.int32), [after, late_fetch], after(edges, to_east)
    )
    late_held = pl.pallas_call(
        late_pack_kernel,
        out_shape=packed_shapes,
        in_specs=[HBM] * 6 + [VMEM] * 6 + [ANY],
        out_specs=(VMEM,) * 6,
        scratch_shapes=buffers + [pltpu.SemaphoreType.DMA((6,))],
        compiler_params=PARAMS,
    )(*in_hbm(*inputs), *early_held, late_mate)
    mirrored_shape = (arrays, rows, cols + LANES)

    def fold(total, third):
        totals = [total, total - 1] + [total - 2] * third
        steps = [(n, 1) for n, t in enumerate(totals) if t % 2 == 0]
        steps += [(n, None) for n, t in enumerate(totals) if t % 2]
        steps += [(n, 0) for n, t in enumerate(totals) if t % 2 == 0]
        used = [[0, 0] for _ in range(3)]
        for at, (n, parity) in enumerate(steps):
            for side in (0, 1):
                if parity in (None, side):
                    used[n][side] = at

        def run(x, place):
            blocks = []
            for n, parity in steps:
                pairs = [
                    (flat(totals[n] - p, top), flat(p, top))
                    for p in around
                    if parity in (None, p % 2)
                ]
                blocks.append(lax.ppermute(x, AXES, pairs))
            return pl.pallas_call(
                functools.partial(fold_kernel, levels, used),
                out_shape=held(*mirrored_shape),
                in_specs=[ANY] + [VMEM] * len(blocks),
                out_specs=VMEM,
                scratch_shapes=[pltpu.SMEM((TILE, LANES), jnp.int32), pltpu.SemaphoreType.DMA],
                compiler_params=PARAMS,
            )(place, *blocks)

        return run

    def at_top(rows_held, place):
        folds = [fold(total, third) for total in around for third in (False, True)]
        return after(lax.switch(place[0, 0], folds, rows_held, place))

    def below(rows_held, place):
        return jnp.zeros(mirrored_shape, jnp.float32)

    mirrored = lax.switch(
        (lax.axis_index("lat") == top).astype(jnp.int32), [below, at_top], early_held[3], after(place, late_mate)
    )

    def near(held_here, east, west):
        _, _, x_rows, y_rows, _, _ = held_here
        return pl.pallas_call(
            near_kernel,
            out_shape=(held(data + 4 * edge, LANES), held(data + 4 * edge + TILE, LANES)),
            in_specs=[VMEM] * 4,
            out_specs=(VMEM,) * 2,
            compiler_params=PARAMS,
        )(x_rows, y_rows, east, west)

    def steps(held_here, x_out, x_in, y_in):
        block, _, _, _, area, root = held_here
        return pl.pallas_call(
            functools.partial(steps_kernel, levels),
            out_shape=held(levels, rows, cols),
            in_specs=[VMEM] * 7,
            out_specs=VMEM,
            scratch_shapes=[pltpu.VMEM((arrays, 3 * rows, cols + LANES), jnp.float32)],
            compiler_params=PARAMS,
        )(block, x_out, x_in, y_in, area, root, mirrored)

    x_out, y_out = near(late_held, even_east, even_west)
    go_east, go_west = join(after(late_held[1], y_out, mirrored), late_mate)
    y_in = lax.ppermute(y_out, AXES, lat_swap(1, 0))
    odd_west = lax.ppermute(go_east, AXES, sent(0, 1))
    odd_east = lax.ppermute(go_west, AXES, sent(0, -1))
    x_in = lax.ppermute(after(x_out, odd_west, odd_east), AXES, lat_swap(0, 0))

    def even_steps(x_out, x_in, y_in, east, west):
        return steps(late_held, x_out, x_in, y_in)

    def odd_steps(x_out, x_in, y_in, east, west):
        x_out, y_out = near(early_held, east, west)
        y_in = lax.ppermute(y_out, AXES, lat_swap(1, 1))
        x_in = lax.ppermute(x_out, AXES, lat_swap(0, 1))
        return steps(early_held, x_out, x_in, y_in)

    return lax.switch(
        odd,
        [even_steps, odd_steps],
        x_out,
        x_in,
        y_in,
        odd_east,
        odd_west,
    )


def solution(mesh):
    return jax.shard_map(
        per_device,
        mesh=mesh,
        in_specs=(
            P(None, "lat", "lon"),
            P(None, "lat", "lon"),
            P(None, "lat", "lon"),
            P(None, "lat", "lon"),
            P("lat", "lon"),
            P("lat", "lon"),
            P(),
        ),
        out_specs=P(None, "lat", "lon"),
        check_vma=False,
    )
```

```python
import functools

import jax
import jax.numpy as jnp
from jax import lax
from jax.experimental import pallas as pl
from jax.experimental.pallas import tpu as pltpu
from jax.sharding import PartitionSpec as P

ITERS = 10
LANES = 128
TILE = 8
PER_ROW = LANES // ITERS
AXES = ("lon", "lat")


def lane_index(rows=TILE):
    return lax.broadcasted_iota(jnp.int32, (rows, LANES), 1)


def slots(arrays):
    places = [(k, t) for k in range(arrays) for t in range(2)]
    return [(k, t, m // PER_ROW, (m % PER_ROW) * ITERS) for m, (k, t) in enumerate(places)]


def early():
    at_top = lax.axis_index("lat") == lax.axis_size("lat") - 1
    return (lax.rem(lax.axis_index("lon"), 2) == 1) | at_top


def pack_kernel(*refs):
    (partner, *sources), outs, place = refs[:7], refs[7:13], refs[13]
    targets, held, arrived = refs[14:20], refs[20], refs[21]
    cols = targets[0].shape[2]

    @pl.when(early())
    def _():
        extra = pltpu.make_async_copy(partner.at[pl.ds(0, held.shape[0])], held, arrived.at[6])
        extra.start()
        pack(sources, targets, arrived, *outs)
        extra.wait()
        moved = held[0] + ITERS
        q = lax.rem(lax.div(moved, cols), lax.axis_size("lon"))
        offset = lax.rem(moved, cols) - ITERS
        branch = 2 * q + jnp.where(offset < ITERS - 1, 1, 0)
        place[...] = jnp.where(lane_index() == 0, branch, offset)


def late_pack_kernel(*refs):
    sources, firsts, outs = refs[:6], refs[6:12], refs[13:19]
    targets, arrived = refs[19:25], refs[25]

    @pl.when(jnp.logical_not(early()))
    def _():
        pack(sources, targets, arrived, *outs)

    @pl.when(early() & (lax.rem(lax.axis_index("lon"), 2) == 0))
    def _():
        for first, out in zip(firsts, outs):
            out[...] = first[...]


def pack(sources, targets, arrived, block, edges, x_rows, y_rows, area_out, root):
    grad, norm, de, dn, area, mask = targets
    levels, rows, cols = grad.shape
    arrays = block.shape[0]
    copies = [
        pltpu.make_async_copy(source, target, arrived.at[n])
        for n, (source, target) in enumerate(zip(sources, targets))
    ]
    for copy in copies:
        copy.start()
    for copy in copies:
        copy.wait()
    block[0:levels] = norm[...] * grad[...]
    block[levels : 2 * levels] = de[...]
    block[2 * levels : 3 * levels] = dn[...]
    block[3 * levels] = mask[...].astype(jnp.float32) / area[...]
    area_out[...] = area[...]
    root[...] = jnp.sqrt(area[...])
    lane = lane_index()
    lat_even = lax.rem(lax.axis_index("lat"), 2) == 0

    def packed(col, first):
        out = {}
        for k, t, row, at in slots(arrays):
            tile = block[k, t * TILE : (t + 1) * TILE, col : col + LANES]
            moved = pltpu.roll(tile, (at - first) % LANES, 1)
            inside = (lane >= at) & (lane < at + ITERS)
            out[row] = jnp.where(inside, moved, out.get(row, jnp.zeros_like(moved)))
        return out

    east, west = packed(cols - LANES, LANES - ITERS), packed(0, 0)
    count = len(east)
    for row in range(count):
        here = slice(row * TILE, (row + 1) * TILE)
        there = slice((count + row) * TILE, (count + row + 1) * TILE)
        edges[here], edges[there] = east[row], west[row]

    sub = lax.broadcasted_iota(jnp.int32, (TILE, LANES), 0)
    for c in range(cols // LANES):
        at = slice(c * LANES, (c + 1) * LANES)
        base = c * (arrays + 2) * TILE
        extra = {}
        for k in range(arrays):
            low, high = block[k, 0:TILE, at], block[k, TILE : 2 * TILE, at]
            here = slice(base + k * TILE, base + (k + 1) * TILE)
            x_rows[here] = jnp.where(lat_even, high, low)
            y_rows[here] = jnp.where(lat_even, low, high)
            lift = 2 * (k % 4)
            inside = (sub >= lift) & (sub < lift + 2)
            north = pltpu.roll(low, (lift + 2) % TILE, 0)
            south = pltpu.roll(high, lift, 0)
            north_held, south_held = extra.get(k // 4, (jnp.zeros_like(low),) * 2)
            extra[k // 4] = (jnp.where(inside, north, north_held), jnp.where(inside, south, south_held))
        for e, (north, south) in extra.items():
            here = slice(base + (arrays + e) * TILE, base + (arrays + e + 1) * TILE)
            x_rows[here] = jnp.where(lat_even, north, south)
            y_rows[here] = jnp.where(lat_even, south, north)


def join_kernel(edges, mate, to_east, to_west):
    half = edges.shape[0] // 2
    low, high = slice(0, half), slice(half, 2 * half)
    to_east[low], to_west[low] = edges[low], edges[high]
    to_east[high], to_west[high] = mate[low], mate[high]


def after_kernel(count, *refs):
    for source, target in zip(refs[:count], refs[-count:]):
        target[...] = source[...]


def after(values, *first):
    values = values if isinstance(values, tuple) else (values,)
    handed = pl.pallas_call(
        functools.partial(after_kernel, len(values)),
        out_shape=tuple(jax.ShapeDtypeStruct(x.shape, x.dtype) for x in values),
        in_specs=[VMEM] * len(values) + [ANY] * len(first),
        out_specs=(VMEM,) * len(values),
        compiler_params=PARAMS,
    )(*values, *first)
    return handed if len(values) > 1 else handed[0]


def near_kernel(x_rows, y_rows, east, west, x_out, y_out):
    rows, tall = x_rows.shape[0], east.shape[0]
    half = tall // 2
    x_out[0:rows] = x_rows[...]
    y_out[0:rows] = y_rows[...]
    x_out[rows : rows + tall] = east[...]
    x_out[rows + tall : rows + 2 * tall] = west[...]
    y_out[rows : rows + half] = east[0:half]
    y_out[rows + half : rows + tall] = west[0:half]
    y_out[rows + tall : y_out.shape[0]] = jnp.zeros((y_out.shape[0] - rows - tall, LANES), jnp.float32)


def reversed_lanes(x):
    index = LANES - 1 - lane_index(x.shape[0])
    return jnp.take_along_axis(x, index, axis=1, mode="promise_in_bounds")


def fold_kernel(levels, used, place, *refs):
    blocks, (out, placed, arrived) = refs[:-3], refs[-3:]
    lon_even = lax.rem(lax.axis_index("lon"), 2) == 0
    copy = pltpu.make_async_copy(place, placed, arrived)
    copy.start()
    arrays, rows, wide = out.shape
    cols = wide - LANES
    tiles_across = cols // LANES
    band = (arrays + 2) * TILE
    copy.wait()
    offset = placed[0, 1]
    span = 3 * cols
    far = lane_index(rows)

    for k in range(arrays):
        east_face = levels <= k < 2 * levels
        north_face = 2 * levels <= k < 3 * levels
        pieces = []
        for even, odd in used:
            for c in range(tiles_across - 1, -1, -1):
                main_at = c * band + k * TILE
                few_at = c * band + (arrays + k // 4) * TILE
                main, few = (
                    jnp.where(lon_even, blocks[even][at : at + TILE], blocks[odd][at : at + TILE])
                    for at in (main_at, few_at)
                )
                few = pltpu.roll(few, (TILE - 2 - 2 * (k % 4)) % TILE, 0)
                pieces.append(reversed_lanes(jnp.concatenate([few, main], axis=0)))
        shift = offset + span - cols + (0 if east_face else 1)
        turned = pltpu.roll(jnp.concatenate(pieces, axis=1), shift, 1)
        beyond = turned[:, cols : cols + LANES]
        before = turned[:, span - LANES :]
        side = jnp.where(far < ITERS, beyond, jnp.where(far >= LANES - ITERS, before, 0.0))
        mirrored = jnp.concatenate([turned[:, :cols], side], axis=1)
        skip = 1 if north_face else 0
        for row in range(rows - 1):
            source = max(rows - 1 - skip - row, 0)
            out[k, row : row + 1] = mirrored[source : source + 1]
        out[k, rows - 1 : rows] = mirrored[rows - 1 : rows]


def steps_kernel(levels, own, x_out, x_in, y_in, area, root, mirrored, out, ext):
    arrays, rows, cols = own.shape
    wide, tall = cols + LANES, 3 * rows
    tiles_across = cols // LANES
    band = (arrays + 2) * TILE
    data = band * tiles_across
    edge = (x_in.shape[0] - data) // 4
    lat = lax.axis_index("lat")
    lat_even = lax.rem(lat, 2) == 0
    at_top = lat == lax.axis_size("lat") - 1
    below_top = lat == lax.axis_size("lat") - 2
    lane = lane_index()

    def put_sides(start, from_east, from_west):
        for k, t, row, at in slots(arrays):
            here = slice(row * TILE, (row + 1) * TILE)
            east = pltpu.roll(from_east[here], (-at) % LANES, 1)
            west = pltpu.roll(from_west[here], (LANES - ITERS - at) % LANES, 1)
            side = jnp.where(lane < ITERS, east, jnp.where(lane >= LANES - ITERS, west, 0.0))
            ext[k, start + t * TILE : start + (t + 1) * TILE, cols:wide] = side

    def put_rows(start, main, spare, lift_base, rows_of):
        for c in range(tiles_across):
            at = slice(c * LANES, (c + 1) * LANES)
            for k in range(arrays):
                base = c * band
                ext[k, start + main * TILE : start + (main + 1) * TILE, at] = rows_of(base + k * TILE)
                few = rows_of(base + (arrays + k // 4) * TILE)
                lift = (lift_base - 2 * (k % 4)) % TILE
                ext[k, start + spare * TILE : start + (spare + 1) * TILE, at] = pltpu.roll(few, lift, 0)

    for k in range(arrays):
        ext[k, rows : 2 * rows, 0:cols] = own[k]
    def part(held, at):
        return held[data + at * edge : data + (at + 1) * edge]

    x_east, x_west = part(x_in, 0), part(x_in, 2)
    y_east, y_west = part(y_in, 0), part(y_in, 1)
    put_sides(
        rows,
        jnp.where(at_top, part(x_in, 1), part(x_out, 0)),
        jnp.where(at_top, part(x_in, 3), part(x_out, 2)),
    )

    def south_rows(at):
        return jnp.where(lat_even, y_in[at : at + TILE], x_in[at : at + TILE])

    def north_rows(at):
        return jnp.where(lat_even, x_in[at : at + TILE], y_in[at : at + TILE])

    put_rows(0, 1, 0, TILE - 2, south_rows)
    put_sides(0, jnp.where(lat_even, y_east, x_east), jnp.where(lat_even, y_west, x_west))

    @pl.when(jnp.logical_not(at_top))
    def _():
        put_rows(2 * rows, 0, 1, 0, north_rows)
        put_sides(
            2 * rows,
            jnp.where(below_top, part(x_out, 1), jnp.where(lat_even, x_east, y_east)),
            jnp.where(below_top, part(x_out, 3), jnp.where(lat_even, x_west, y_west)),
        )

    @pl.when(at_top)
    def _():
        for k in range(arrays):
            ext[k, 2 * rows : 3 * rows] = mirrored[k]
        for k in range(2 * levels, 3 * levels):
            face = ext[k, 2 * rows - 1 : 2 * rows]
            ext[k, 2 * rows - 1 : 2 * rows] = 0.5 * (face + mirrored[k, rows - 1 : rows])

    def east_of(x):
        return pltpu.roll(x, wide - 1, 1)

    def west_of(x):
        return pltpu.roll(x, 1, 1)

    def north_of(x):
        return pltpu.roll(x, x.shape[0] - 1, 0)

    def south_of(x):
        return pltpu.roll(x, 1, 0)

    weight = ext[3 * levels]
    sea = jnp.where(weight > 0.0, 1.0, 0.0)
    sea_east = sea * east_of(sea)
    sea_north = sea * north_of(sea)
    inner = slice(TILE, tall - TILE)
    coefs, values = [], []
    for level in range(levels):
        east = ext[levels + level] * sea_east
        north = ext[2 * levels + level] * sea_north
        west, south = west_of(east), south_of(north)
        rest = 1.0 - weight * ((east + west) + (north + south))
        coefs.append([rest] + [weight * x for x in (east, west, north, south)])
        values.append(weight * ext[level])
    for turn in range(ITERS):
        for level in range(levels):
            u = values[level]
            rest, east, west, north, south = coefs[level]
            u = (rest * u + (east * east_of(u) + west * west_of(u))) + (
                north * north_of(u) + south * south_of(u)
            )
            if turn == 1:
                u = u[inner]
                coefs[level] = [x[inner] for x in coefs[level]]
            values[level] = u
    start = rows - TILE
    own_weight = weight[rows : 2 * rows, :cols]
    for level in range(levels):
        u = values[level][start : start + rows, :cols]
        state = jnp.where(own_weight > 0.0, u * area[...], own[level])
        out[level] = state / root[...]


VMEM = pl.BlockSpec(memory_space=pltpu.VMEM)
SMEM = pl.BlockSpec(memory_space=pltpu.SMEM)
ANY = pl.BlockSpec(memory_space=pl.ANY)
HBM = pl.BlockSpec(memory_space=pltpu.HBM)
PARAMS = pltpu.CompilerParams(vmem_limit_bytes=8 * 1024 * 1024)


def per_device(gradient, norm_factor, diff_east, diff_north, cell_area, sea_mask, partner):
    levels, rows, cols = gradient.shape
    arrays = 3 * levels + 1
    lon_count, lat_count = lax.axis_size("lon"), lax.axis_size("lat")

    def held(*shape):
        return jax.ShapeDtypeStruct(shape, jnp.float32)

    inputs = (gradient, norm_factor, diff_east, diff_north, cell_area, sea_mask)
    edge = (slots(arrays)[-1][2] + 1) * TILE
    data = (arrays + 2) * TILE * (cols // LANES)
    def flat(lon, lat):
        return (lon % lon_count) * lat_count + lat

    top = lat_count - 1
    around = range(lon_count)

    def swap(pairs):
        return [pair for a, b in pairs for pair in ((a, b), (b, a))]

    def sent(start, step):
        return [(flat(p, i), flat(p + step, i)) for p in around[start::2] for i in range(top)]

    def lat_swap(start, parity):
        return swap(
            [(flat(p, i), flat(p, i + 1)) for p in around[parity::2] for i in range(start, top, 2)]
        )

    def mirror(total):
        return [(flat(total - p, top), flat(p, top)) for p in around]

    packed_shapes = (
        held(arrays, rows, cols),
        held(2 * edge, LANES),
        held(data, LANES),
        held(data, LANES),
        held(rows, cols),
        held(rows, cols),
    )
    joined_shapes = (held(2 * edge, LANES),) * 2
    odd = lax.rem(lax.axis_index("lon"), 2)

    def join(edges, mate):
        return pl.pallas_call(
            join_kernel,
            out_shape=joined_shapes,
            in_specs=[VMEM] * 2,
            out_specs=(VMEM,) * 2,
            compiler_params=PARAMS,
        )(edges, mate)

    def in_hbm(*arrays):
        return [pltpu.with_memory_space_constraint(x, pltpu.HBM) for x in arrays]

    buffers = [pltpu.VMEM(x.shape, x.dtype) for x in inputs]
    *early_held, place = pl.pallas_call(
        pack_kernel,
        out_shape=packed_shapes + (jax.ShapeDtypeStruct((TILE, LANES), jnp.int32),),
        in_specs=[HBM] * 7,
        out_specs=(VMEM,) * 7,
        scratch_shapes=buffers
        + [pltpu.SMEM((LANES,), jnp.int32), pltpu.SemaphoreType.DMA((7,))],
        compiler_params=PARAMS,
    )(*in_hbm(partner, *inputs))

    def mates(parity):
        return [(flat(p, top), flat(p, top - 1)) for p in around[parity::2]]

    def fetch(edges):
        return join(edges, lax.ppermute(edges, AXES, mates(1)))

    def no_fetch(edges):
        return join(edges, edges)

    near_top = lax.axis_index("lat") >= top - 1
    edges = early_held[1]
    to_east, to_west = lax.switch(
        (near_top & (odd == 1)).astype(jnp.int32), [no_fetch, fetch], edges
    )
    even_east = lax.ppermute(to_west, AXES, sent(1, -1))
    even_west = lax.ppermute(to_east, AXES, sent(1, 1))

    def late_fetch(edges):
        return after(lax.ppermute(edges, AXES, mates(0)))

    late_mate = lax.switch(
        (near_top & (odd == 0)).astype(jnp.int32), [after, late_fetch], after(edges, to_east)
    )
    late_held = pl.pallas_call(
        late_pack_kernel,
        out_shape=packed_shapes,
        in_specs=[HBM] * 6 + [VMEM] * 6 + [ANY],
        out_specs=(VMEM,) * 6,
        scratch_shapes=buffers + [pltpu.SemaphoreType.DMA((6,))],
        compiler_params=PARAMS,
    )(*in_hbm(*inputs), *early_held, late_mate)
    mirrored_shape = (arrays, rows, cols + LANES)

    def fold(total, third):
        totals = [total, total - 1] + [total - 2] * third
        steps = [(n, None) for n in sorted(range(len(totals)), key=lambda n: totals[n] % 2)]
        used = [[0, 0] for _ in range(3)]
        for at, (n, parity) in enumerate(steps):
            for side in (0, 1):
                if parity in (None, side):
                    used[n][side] = at

        def run(x, place):
            blocks = []
            for n, parity in steps:
                pairs = [
                    (flat(totals[n] - p, top), flat(p, top))
                    for p in around
                    if parity in (None, p % 2)
                ]
                blocks.append(lax.ppermute(x, AXES, pairs))
            return pl.pallas_call(
                functools.partial(fold_kernel, levels, used),
                out_shape=held(*mirrored_shape),
                in_specs=[ANY] + [VMEM] * len(blocks),
                out_specs=VMEM,
                scratch_shapes=[pltpu.SMEM((TILE, LANES), jnp.int32), pltpu.SemaphoreType.DMA],
                compiler_params=PARAMS,
            )(place, *blocks)

        return run

    def at_top(rows_held, place):
        folds = [fold(total, third) for total in around for third in (False, True)]
        return after(lax.switch(place[0, 0], folds, rows_held, place))

    def below(rows_held, place):
        return jnp.zeros(mirrored_shape, jnp.float32)

    mirrored = lax.switch(
        (lax.axis_index("lat") == top).astype(jnp.int32), [below, at_top], early_held[3], after(place, late_mate)
    )

    def near(held_here, east, west):
        _, _, x_rows, y_rows, _, _ = held_here
        return pl.pallas_call(
            near_kernel,
            out_shape=(held(data + 4 * edge, LANES), held(data + 4 * edge + TILE, LANES)),
            in_specs=[VMEM] * 4,
            out_specs=(VMEM,) * 2,
            compiler_params=PARAMS,
        )(x_rows, y_rows, east, west)

    def steps(held_here, x_out, x_in, y_in):
        block, _, _, _, area, root = held_here
        return pl.pallas_call(
            functools.partial(steps_kernel, levels),
            out_shape=held(levels, rows, cols),
            in_specs=[VMEM] * 7,
            out_specs=VMEM,
            scratch_shapes=[pltpu.VMEM((arrays, 3 * rows, cols + LANES), jnp.float32)],
            compiler_params=PARAMS,
        )(block, x_out, x_in, y_in, area, root, mirrored)

    x_out, y_out = near(late_held, even_east, even_west)
    go_east, go_west = join(after(late_held[1], y_out, mirrored), late_mate)
    y_in = lax.ppermute(y_out, AXES, lat_swap(1, 0))
    odd_west = lax.ppermute(go_east, AXES, sent(0, 1))
    odd_east = lax.ppermute(go_west, AXES, sent(0, -1))
    x_in = lax.ppermute(after(x_out, odd_west, odd_east), AXES, lat_swap(0, 0))

    def even_steps(x_out, x_in, y_in, east, west):
        return steps(late_held, x_out, x_in, y_in)

    def odd_steps(x_out, x_in, y_in, east, west):
        x_out, y_out = near(early_held, east, west)
        y_in = lax.ppermute(y_out, AXES, lat_swap(1, 1))
        x_in = lax.ppermute(x_out, AXES, lat_swap(0, 1))
        return steps(early_held, x_out, x_in, y_in)

    return lax.switch(
        odd,
        [even_steps, odd_steps],
        x_out,
        x_in,
        y_in,
        odd_east,
        odd_west,
    )


def solution(mesh):
    return jax.shard_map(
        per_device,
        mesh=mesh,
        in_specs=(
            P(None, "lat", "lon"),
            P(None, "lat", "lon"),
            P(None, "lat", "lon"),
            P(None, "lat", "lon"),
            P("lat", "lon"),
            P("lat", "lon"),
            P(),
        ),
        out_specs=P(None, "lat", "lon"),
        check_vma=False,
    )
```

```python
import functools

import jax
import jax.numpy as jnp
from jax import lax
from jax.experimental import pallas as pl
from jax.experimental.pallas import tpu as pltpu
from jax.sharding import PartitionSpec as P

ITERS = 10
LANES = 128
TILE = 8
PER_ROW = LANES // ITERS
AXES = ("lon", "lat")


def lane_index(rows=TILE):
    return lax.broadcasted_iota(jnp.int32, (rows, LANES), 1)


def slots(arrays):
    places = [(k, t) for k in range(arrays) for t in range(2)]
    return [(k, t, m // PER_ROW, (m % PER_ROW) * ITERS) for m, (k, t) in enumerate(places)]


def early():
    at_top = lax.axis_index("lat") == lax.axis_size("lat") - 1
    return (lax.rem(lax.axis_index("lon"), 2) == 1) | at_top


def pack_kernel(*refs):
    (partner, *sources), outs, place = refs[:7], refs[7:13], refs[13]
    targets, held, arrived = refs[14:20], refs[20], refs[21]
    cols = targets[0].shape[2]

    @pl.when(early())
    def _():
        extra = pltpu.make_async_copy(partner.at[pl.ds(0, held.shape[0])], held, arrived.at[6])
        extra.start()
        pack(sources, targets, arrived, *outs)
        extra.wait()
        moved = held[0] + ITERS
        q = lax.rem(lax.div(moved, cols), lax.axis_size("lon"))
        offset = lax.rem(moved, cols) - ITERS
        branch = 2 * q + jnp.where(offset < ITERS - 1, 1, 0)
        place[...] = jnp.where(lane_index() == 0, branch, offset)


def late_pack_kernel(*refs):
    sources, firsts, outs = refs[:6], refs[6:12], refs[13:19]
    targets, arrived = refs[19:25], refs[25]

    @pl.when(jnp.logical_not(early()))
    def _():
        pack(sources, targets, arrived, *outs)

    @pl.when(early() & (lax.rem(lax.axis_index("lon"), 2) == 0))
    def _():
        for first, out in zip(firsts, outs):
            out[...] = first[...]


def pack(sources, targets, arrived, block, edges, x_rows, y_rows, area_out, root):
    grad, norm, de, dn, area, mask = targets
    levels, rows, cols = grad.shape
    arrays = block.shape[0]
    copies = [
        pltpu.make_async_copy(source, target, arrived.at[n])
        for n, (source, target) in enumerate(zip(sources, targets))
    ]
    for copy in copies:
        copy.start()
    for copy in copies:
        copy.wait()
    block[0:levels] = norm[...] * grad[...]
    block[levels : 2 * levels] = de[...]
    block[2 * levels : 3 * levels] = dn[...]
    block[3 * levels] = mask[...].astype(jnp.float32) / area[...]
    area_out[...] = area[...]
    root[...] = jnp.sqrt(area[...])
    lane = lane_index()
    lat_even = lax.rem(lax.axis_index("lat"), 2) == 0

    def packed(col, first):
        out = {}
        for k, t, row, at in slots(arrays):
            tile = block[k, t * TILE : (t + 1) * TILE, col : col + LANES]
            moved = pltpu.roll(tile, (at - first) % LANES, 1)
            inside = (lane >= at) & (lane < at + ITERS)
            out[row] = jnp.where(inside, moved, out.get(row, jnp.zeros_like(moved)))
        return out

    east, west = packed(cols - LANES, LANES - ITERS), packed(0, 0)
    count = len(east)
    for row in range(count):
        here = slice(row * TILE, (row + 1) * TILE)
        there = slice((count + row) * TILE, (count + row + 1) * TILE)
        edges[here], edges[there] = east[row], west[row]

    sub = lax.broadcasted_iota(jnp.int32, (TILE, LANES), 0)
    for c in range(cols // LANES):
        at = slice(c * LANES, (c + 1) * LANES)
        base = c * (arrays + 2) * TILE
        extra = {}
        for k in range(arrays):
            low, high = block[k, 0:TILE, at], block[k, TILE : 2 * TILE, at]
            here = slice(base + k * TILE, base + (k + 1) * TILE)
            x_rows[here] = jnp.where(lat_even, high, low)
            y_rows[here] = jnp.where(lat_even, low, high)
            lift = 2 * (k % 4)
            inside = (sub >= lift) & (sub < lift + 2)
            north = pltpu.roll(low, (lift + 2) % TILE, 0)
            south = pltpu.roll(high, lift, 0)
            north_held, south_held = extra.get(k // 4, (jnp.zeros_like(low),) * 2)
            extra[k // 4] = (jnp.where(inside, north, north_held), jnp.where(inside, south, south_held))
        for e, (north, south) in extra.items():
            here = slice(base + (arrays + e) * TILE, base + (arrays + e + 1) * TILE)
            x_rows[here] = jnp.where(lat_even, north, south)
            y_rows[here] = jnp.where(lat_even, south, north)


def join_kernel(edges, mate, to_east, to_west):
    half = edges.shape[0] // 2
    low, high = slice(0, half), slice(half, 2 * half)
    to_east[low], to_west[low] = edges[low], edges[high]
    to_east[high], to_west[high] = mate[low], mate[high]


def after_kernel(count, *refs):
    for source, target in zip(refs[:count], refs[-count:]):
        target[...] = source[...]


def after(values, *first):
    values = values if isinstance(values, tuple) else (values,)
    handed = pl.pallas_call(
        functools.partial(after_kernel, len(values)),
        out_shape=tuple(jax.ShapeDtypeStruct(x.shape, x.dtype) for x in values),
        in_specs=[VMEM] * len(values) + [ANY] * len(first),
        out_specs=(VMEM,) * len(values),
        compiler_params=PARAMS,
    )(*values, *first)
    return handed if len(values) > 1 else handed[0]


def near_kernel(x_rows, y_rows, east, west, x_out, y_out):
    rows, tall = x_rows.shape[0], east.shape[0]
    half = tall // 2
    x_out[0:rows] = x_rows[...]
    y_out[0:rows] = y_rows[...]
    x_out[rows : rows + tall] = east[...]
    x_out[rows + tall : rows + 2 * tall] = west[...]
    y_out[rows : rows + half] = east[0:half]
    y_out[rows + half : rows + tall] = west[0:half]
    y_out[rows + tall : y_out.shape[0]] = jnp.zeros((y_out.shape[0] - rows - tall, LANES), jnp.float32)


def reversed_lanes(x):
    index = LANES - 1 - lane_index(x.shape[0])
    return jnp.take_along_axis(x, index, axis=1, mode="promise_in_bounds")


def fold_kernel(levels, used, place, *refs):
    blocks, (out, placed, arrived) = refs[:-3], refs[-3:]
    lon_even = lax.rem(lax.axis_index("lon"), 2) == 0
    copy = pltpu.make_async_copy(place, placed, arrived)
    copy.start()
    arrays, rows, wide = out.shape
    cols = wide - LANES
    tiles_across = cols // LANES
    band = (arrays + 2) * TILE
    copy.wait()
    offset = placed[0, 1]
    span = 3 * cols
    far = lane_index(rows)

    for k in range(arrays):
        east_face = levels <= k < 2 * levels
        north_face = 2 * levels <= k < 3 * levels
        pieces = []
        for even, odd in used:
            for c in range(tiles_across - 1, -1, -1):
                main_at = c * band + k * TILE
                few_at = c * band + (arrays + k // 4) * TILE
                main, few = (
                    jnp.where(lon_even, blocks[even][at : at + TILE], blocks[odd][at : at + TILE])
                    for at in (main_at, few_at)
                )
                few = pltpu.roll(few, (TILE - 2 - 2 * (k % 4)) % TILE, 0)
                pieces.append(reversed_lanes(jnp.concatenate([few, main], axis=0)))
        shift = offset + span - cols + (0 if east_face else 1)
        turned = pltpu.roll(jnp.concatenate(pieces, axis=1), shift, 1)
        beyond = turned[:, cols : cols + LANES]
        before = turned[:, span - LANES :]
        side = jnp.where(far < ITERS, beyond, jnp.where(far >= LANES - ITERS, before, 0.0))
        mirrored = jnp.concatenate([turned[:, :cols], side], axis=1)
        skip = 1 if north_face else 0
        for row in range(rows - 1):
            source = max(rows - 1 - skip - row, 0)
            out[k, row : row + 1] = mirrored[source : source + 1]
        out[k, rows - 1 : rows] = mirrored[rows - 1 : rows]


def steps_kernel(levels, own, x_out, x_in, y_in, area, root, mirrored, out, ext):
    arrays, rows, cols = own.shape
    wide, tall = cols + LANES, 3 * rows
    tiles_across = cols // LANES
    band = (arrays + 2) * TILE
    data = band * tiles_across
    edge = (x_in.shape[0] - data) // 4
    lat = lax.axis_index("lat")
    lat_even = lax.rem(lat, 2) == 0
    at_top = lat == lax.axis_size("lat") - 1
    below_top = lat == lax.axis_size("lat") - 2
    lane = lane_index()

    def put_sides(start, from_east, from_west):
        for k, t, row, at in slots(arrays):
            here = slice(row * TILE, (row + 1) * TILE)
            east = pltpu.roll(from_east[here], (-at) % LANES, 1)
            west = pltpu.roll(from_west[here], (LANES - ITERS - at) % LANES, 1)
            side = jnp.where(lane < ITERS, east, jnp.where(lane >= LANES - ITERS, west, 0.0))
            ext[k, start + t * TILE : start + (t + 1) * TILE, cols:wide] = side

    def put_rows(start, main, spare, lift_base, rows_of):
        for c in range(tiles_across):
            at = slice(c * LANES, (c + 1) * LANES)
            for k in range(arrays):
                base = c * band
                ext[k, start + main * TILE : start + (main + 1) * TILE, at] = rows_of(base + k * TILE)
                few = rows_of(base + (arrays + k // 4) * TILE)
                lift = (lift_base - 2 * (k % 4)) % TILE
                ext[k, start + spare * TILE : start + (spare + 1) * TILE, at] = pltpu.roll(few, lift, 0)

    for k in range(arrays):
        ext[k, rows : 2 * rows, 0:cols] = own[k]
    def part(held, at):
        return held[data + at * edge : data + (at + 1) * edge]

    x_east, x_west = part(x_in, 0), part(x_in, 2)
    y_east, y_west = part(y_in, 0), part(y_in, 1)
    put_sides(
        rows,
        jnp.where(at_top, part(x_in, 1), part(x_out, 0)),
        jnp.where(at_top, part(x_in, 3), part(x_out, 2)),
    )

    def south_rows(at):
        return jnp.where(lat_even, y_in[at : at + TILE], x_in[at : at + TILE])

    def north_rows(at):
        return jnp.where(lat_even, x_in[at : at + TILE], y_in[at : at + TILE])

    put_rows(0, 1, 0, TILE - 2, south_rows)
    put_sides(0, jnp.where(lat_even, y_east, x_east), jnp.where(lat_even, y_west, x_west))

    @pl.when(jnp.logical_not(at_top))
    def _():
        put_rows(2 * rows, 0, 1, 0, north_rows)
        put_sides(
            2 * rows,
            jnp.where(below_top, part(x_out, 1), jnp.where(lat_even, x_east, y_east)),
            jnp.where(below_top, part(x_out, 3), jnp.where(lat_even, x_west, y_west)),
        )

    @pl.when(at_top)
    def _():
        for k in range(arrays):
            ext[k, 2 * rows : 3 * rows] = mirrored[k]
        for k in range(2 * levels, 3 * levels):
            face = ext[k, 2 * rows - 1 : 2 * rows]
            ext[k, 2 * rows - 1 : 2 * rows] = 0.5 * (face + mirrored[k, rows - 1 : rows])

    def east_of(x):
        return pltpu.roll(x, wide - 1, 1)

    def west_of(x):
        return pltpu.roll(x, 1, 1)

    def north_of(x):
        return pltpu.roll(x, x.shape[0] - 1, 0)

    def south_of(x):
        return pltpu.roll(x, 1, 0)

    weight = ext[3 * levels]
    sea = jnp.where(weight > 0.0, 1.0, 0.0)
    sea_east = sea * east_of(sea)
    sea_north = sea * north_of(sea)
    inner = slice(TILE, tall - TILE)
    coefs, values = [], []
    for level in range(levels):
        east = ext[levels + level] * sea_east
        north = ext[2 * levels + level] * sea_north
        west, south = west_of(east), south_of(north)
        rest = 1.0 - weight * ((east + west) + (north + south))
        coefs.append([rest] + [weight * x for x in (east, west, north, south)])
        values.append(weight * ext[level])
    for turn in range(ITERS):
        for level in range(levels):
            u = values[level]
            rest, east, west, north, south = coefs[level]
            u = (rest * u + (east * east_of(u) + west * west_of(u))) + (
                north * north_of(u) + south * south_of(u)
            )
            if turn == 1:
                u = u[inner]
                coefs[level] = [x[inner] for x in coefs[level]]
            values[level] = u
    start = rows - TILE
    own_weight = weight[rows : 2 * rows, :cols]
    for level in range(levels):
        u = values[level][start : start + rows, :cols]
        state = jnp.where(own_weight > 0.0, u * area[...], own[level])
        out[level] = state / root[...]


VMEM = pl.BlockSpec(memory_space=pltpu.VMEM)
SMEM = pl.BlockSpec(memory_space=pltpu.SMEM)
ANY = pl.BlockSpec(memory_space=pl.ANY)
HBM = pl.BlockSpec(memory_space=pltpu.HBM)
PARAMS = pltpu.CompilerParams(vmem_limit_bytes=8 * 1024 * 1024)


def per_device(gradient, norm_factor, diff_east, diff_north, cell_area, sea_mask, partner):
    levels, rows, cols = gradient.shape
    arrays = 3 * levels + 1
    lon_count, lat_count = lax.axis_size("lon"), lax.axis_size("lat")

    def held(*shape):
        return jax.ShapeDtypeStruct(shape, jnp.float32)

    inputs = (gradient, norm_factor, diff_east, diff_north, cell_area, sea_mask)
    edge = (slots(arrays)[-1][2] + 1) * TILE
    data = (arrays + 2) * TILE * (cols // LANES)
    def flat(lon, lat):
        return (lon % lon_count) * lat_count + lat

    top = lat_count - 1
    around = range(lon_count)

    def swap(pairs):
        return [pair for a, b in pairs for pair in ((a, b), (b, a))]

    def sent(start, step):
        return [(flat(p, i), flat(p + step, i)) for p in around[start::2] for i in range(top)]

    def lat_swap(start, parity):
        return swap(
            [(flat(p, i), flat(p, i + 1)) for p in around[parity::2] for i in range(start, top, 2)]
        )

    def mirror(total):
        return [(flat(total - p, top), flat(p, top)) for p in around]

    packed_shapes = (
        held(arrays, rows, cols),
        held(2 * edge, LANES),
        held(data, LANES),
        held(data, LANES),
        held(rows, cols),
        held(rows, cols),
    )
    joined_shapes = (held(2 * edge, LANES),) * 2
    odd = lax.rem(lax.axis_index("lon"), 2)

    def join(edges, mate):
        return pl.pallas_call(
            join_kernel,
            out_shape=joined_shapes,
            in_specs=[VMEM] * 2,
            out_specs=(VMEM,) * 2,
            compiler_params=PARAMS,
        )(edges, mate)

    def in_hbm(*arrays):
        return [pltpu.with_memory_space_constraint(x, pltpu.HBM) for x in arrays]

    buffers = [pltpu.VMEM(x.shape, x.dtype) for x in inputs]
    *early_held, place = pl.pallas_call(
        pack_kernel,
        out_shape=packed_shapes + (jax.ShapeDtypeStruct((TILE, LANES), jnp.int32),),
        in_specs=[HBM] * 7,
        out_specs=(VMEM,) * 7,
        scratch_shapes=buffers
        + [pltpu.SMEM((LANES,), jnp.int32), pltpu.SemaphoreType.DMA((7,))],
        compiler_params=PARAMS,
    )(*in_hbm(partner, *inputs))

    def mates(parity):
        return [(flat(p, top), flat(p, top - 1)) for p in around[parity::2]]

    def fetch(edges):
        return join(edges, lax.ppermute(edges, AXES, mates(1)))

    def no_fetch(edges):
        return join(edges, edges)

    near_top = lax.axis_index("lat") >= top - 1
    edges = early_held[1]
    to_east, to_west = lax.switch(
        (near_top & (odd == 1)).astype(jnp.int32), [no_fetch, fetch], edges
    )
    even_east = lax.ppermute(to_west, AXES, sent(1, -1))
    even_west = lax.ppermute(to_east, AXES, sent(1, 1))

    def late_fetch(edges):
        return after(lax.ppermute(edges, AXES, mates(0)))

    late_mate = lax.switch(
        (near_top & (odd == 0)).astype(jnp.int32), [after, late_fetch], after(edges, to_west)
    )
    late_held = pl.pallas_call(
        late_pack_kernel,
        out_shape=packed_shapes,
        in_specs=[HBM] * 6 + [VMEM] * 6 + [ANY],
        out_specs=(VMEM,) * 6,
        scratch_shapes=buffers + [pltpu.SemaphoreType.DMA((6,))],
        compiler_params=PARAMS,
    )(*in_hbm(*inputs), *early_held, late_mate)
    mirrored_shape = (arrays, rows, cols + LANES)

    def fold(total, third):
        totals = [total, total - 1] + [total - 2] * third
        steps = [(n, None) for n in sorted(range(len(totals)), key=lambda n: totals[n] % 2)]
        used = [[0, 0] for _ in range(3)]
        for at, (n, parity) in enumerate(steps):
            for side in (0, 1):
                if parity in (None, side):
                    used[n][side] = at

        def run(x, place):
            blocks = []
            for n, parity in steps:
                pairs = [
                    (flat(totals[n] - p, top), flat(p, top))
                    for p in around
                    if parity in (None, p % 2)
                ]
                blocks.append(lax.ppermute(x, AXES, pairs))
            return pl.pallas_call(
                functools.partial(fold_kernel, levels, used),
                out_shape=held(*mirrored_shape),
                in_specs=[ANY] + [VMEM] * len(blocks),
                out_specs=VMEM,
                scratch_shapes=[pltpu.SMEM((TILE, LANES), jnp.int32), pltpu.SemaphoreType.DMA],
                compiler_params=PARAMS,
            )(place, *blocks)

        return run

    def at_top(rows_held, place):
        folds = [fold(total, third) for total in around for third in (False, True)]
        return after(lax.switch(place[0, 0], folds, rows_held, place))

    def below(rows_held, place):
        return jnp.zeros(mirrored_shape, jnp.float32)

    mirrored = lax.switch(
        (lax.axis_index("lat") == top).astype(jnp.int32), [below, at_top], early_held[3], after(place, late_mate)
    )

    def near(held_here, east, west):
        _, _, x_rows, y_rows, _, _ = held_here
        return pl.pallas_call(
            near_kernel,
            out_shape=(held(data + 4 * edge, LANES), held(data + 4 * edge + TILE, LANES)),
            in_specs=[VMEM] * 4,
            out_specs=(VMEM,) * 2,
            compiler_params=PARAMS,
        )(x_rows, y_rows, east, west)

    def steps(held_here, x_out, x_in, y_in):
        block, _, _, _, area, root = held_here
        return pl.pallas_call(
            functools.partial(steps_kernel, levels),
            out_shape=held(levels, rows, cols),
            in_specs=[VMEM] * 7,
            out_specs=VMEM,
            scratch_shapes=[pltpu.VMEM((arrays, 3 * rows, cols + LANES), jnp.float32)],
            compiler_params=PARAMS,
        )(block, x_out, x_in, y_in, area, root, mirrored)

    x_out, y_out = near(late_held, even_east, even_west)
    go_east, go_west = join(after(late_held[1], y_out, mirrored), late_mate)
    y_in = lax.ppermute(y_out, AXES, lat_swap(1, 0))
    odd_west = lax.ppermute(go_east, AXES, sent(0, 1))
    odd_east = lax.ppermute(go_west, AXES, sent(0, -1))
    x_in = lax.ppermute(after(x_out, odd_east, odd_west), AXES, lat_swap(0, 0))

    def even_steps(x_out, x_in, y_in, east, west):
        return steps(late_held, x_out, x_in, y_in)

    def odd_steps(x_out, x_in, y_in, east, west):
        x_out, y_out = near(early_held, east, west)
        y_in = lax.ppermute(y_out, AXES, lat_swap(1, 1))
        x_in = lax.ppermute(x_out, AXES, lat_swap(0, 1))
        return steps(early_held, x_out, x_in, y_in)

    return lax.switch(
        odd,
        [even_steps, odd_steps],
        x_out,
        x_in,
        y_in,
        odd_east,
        odd_west,
    )


def solution(mesh):
    return jax.shard_map(
        per_device,
        mesh=mesh,
        in_specs=(
            P(None, "lat", "lon"),
            P(None, "lat", "lon"),
            P(None, "lat", "lon"),
            P(None, "lat", "lon"),
            P("lat", "lon"),
            P("lat", "lon"),
            P(),
        ),
        out_specs=P(None, "lat", "lon"),
        check_vma=False,
    )
```

```python
import functools

import jax
import jax.numpy as jnp
from jax import lax
from jax.experimental import pallas as pl
from jax.experimental.pallas import tpu as pltpu
from jax.sharding import PartitionSpec as P

ITERS = 10
LANES = 128
TILE = 8
PER_ROW = LANES // ITERS
AXES = ("lon", "lat")


def lane_index(rows=TILE):
    return lax.broadcasted_iota(jnp.int32, (rows, LANES), 1)


def slots(arrays):
    places = [(k, t) for k in range(arrays) for t in range(2)]
    return [(k, t, m // PER_ROW, (m % PER_ROW) * ITERS) for m, (k, t) in enumerate(places)]


def early():
    at_top = lax.axis_index("lat") == lax.axis_size("lat") - 1
    return (lax.rem(lax.axis_index("lon"), 2) == 1) | at_top


def pack_kernel(*refs):
    (partner, *sources), outs, place = refs[:7], refs[7:13], refs[13]
    targets, held, arrived = refs[14:20], refs[20], refs[21]
    cols = targets[0].shape[2]

    @pl.when(early())
    def _():
        extra = pltpu.make_async_copy(partner.at[pl.ds(0, held.shape[0])], held, arrived.at[6])
        extra.start()
        pack(sources, targets, arrived, *outs)
        extra.wait()
        moved = held[0] + ITERS
        q = lax.rem(lax.div(moved, cols), lax.axis_size("lon"))
        offset = lax.rem(moved, cols) - ITERS
        branch = 2 * q + jnp.where(offset < ITERS - 1, 1, 0)
        place[...] = jnp.where(lane_index() == 0, branch, offset)


def late_pack_kernel(*refs):
    sources, firsts, outs = refs[:6], refs[6:12], refs[13:19]
    targets, arrived = refs[19:25], refs[25]

    @pl.when(jnp.logical_not(early()))
    def _():
        pack(sources, targets, arrived, *outs)

    @pl.when(early() & (lax.rem(lax.axis_index("lon"), 2) == 0))
    def _():
        for first, out in zip(firsts, outs):
            out[...] = first[...]


def pack(sources, targets, arrived, block, edges, x_rows, y_rows, area_out, root):
    grad, norm, de, dn, area, mask = targets
    levels, rows, cols = grad.shape
    arrays = block.shape[0]
    copies = [
        pltpu.make_async_copy(source, target, arrived.at[n])
        for n, (source, target) in enumerate(zip(sources, targets))
    ]
    for copy in copies:
        copy.start()
    for copy in copies:
        copy.wait()
    block[0:levels] = norm[...] * grad[...]
    block[levels : 2 * levels] = de[...]
    block[2 * levels : 3 * levels] = dn[...]
    block[3 * levels] = mask[...].astype(jnp.float32) / area[...]
    area_out[...] = area[...]
    root[...] = jnp.sqrt(area[...])
    lane = lane_index()
    lat_even = lax.rem(lax.axis_index("lat"), 2) == 0

    def packed(col, first):
        out = {}
        for k, t, row, at in slots(arrays):
            tile = block[k, t * TILE : (t + 1) * TILE, col : col + LANES]
            moved = pltpu.roll(tile, (at - first) % LANES, 1)
            inside = (lane >= at) & (lane < at + ITERS)
            out[row] = jnp.where(inside, moved, out.get(row, jnp.zeros_like(moved)))
        return out

    east, west = packed(cols - LANES, LANES - ITERS), packed(0, 0)
    count = len(east)
    for row in range(count):
        here = slice(row * TILE, (row + 1) * TILE)
        there = slice((count + row) * TILE, (count + row + 1) * TILE)
        edges[here], edges[there] = east[row], west[row]

    sub = lax.broadcasted_iota(jnp.int32, (TILE, LANES), 0)
    for c in range(cols // LANES):
        at = slice(c * LANES, (c + 1) * LANES)
        base = c * (arrays + 2) * TILE
        extra = {}
        for k in range(arrays):
            low, high = block[k, 0:TILE, at], block[k, TILE : 2 * TILE, at]
            here = slice(base + k * TILE, base + (k + 1) * TILE)
            x_rows[here] = jnp.where(lat_even, high, low)
            y_rows[here] = jnp.where(lat_even, low, high)
            lift = 2 * (k % 4)
            inside = (sub >= lift) & (sub < lift + 2)
            north = pltpu.roll(low, (lift + 2) % TILE, 0)
            south = pltpu.roll(high, lift, 0)
            north_held, south_held = extra.get(k // 4, (jnp.zeros_like(low),) * 2)
            extra[k // 4] = (jnp.where(inside, north, north_held), jnp.where(inside, south, south_held))
        for e, (north, south) in extra.items():
            here = slice(base + (arrays + e) * TILE, base + (arrays + e + 1) * TILE)
            x_rows[here] = jnp.where(lat_even, north, south)
            y_rows[here] = jnp.where(lat_even, south, north)


def join_kernel(edges, mate, to_east, to_west):
    half = edges.shape[0] // 2
    low, high = slice(0, half), slice(half, 2 * half)
    to_east[low], to_west[low] = edges[low], edges[high]
    to_east[high], to_west[high] = mate[low], mate[high]


def after_kernel(count, *refs):
    for source, target in zip(refs[:count], refs[-count:]):
        target[...] = source[...]


def after(values, *first):
    values = values if isinstance(values, tuple) else (values,)
    handed = pl.pallas_call(
        functools.partial(after_kernel, len(values)),
        out_shape=tuple(jax.ShapeDtypeStruct(x.shape, x.dtype) for x in values),
        in_specs=[VMEM] * len(values) + [ANY] * len(first),
        out_specs=(VMEM,) * len(values),
        compiler_params=PARAMS,
    )(*values, *first)
    return handed if len(values) > 1 else handed[0]


def near_kernel(x_rows, y_rows, east, west, x_out, y_out):
    rows, tall = x_rows.shape[0], east.shape[0]
    half = tall // 2
    x_out[0:rows] = x_rows[...]
    y_out[0:rows] = y_rows[...]
    x_out[rows : rows + tall] = east[...]
    x_out[rows + tall : rows + 2 * tall] = west[...]
    y_out[rows : rows + half] = east[0:half]
    y_out[rows + half : rows + tall] = west[0:half]
    y_out[rows + tall : y_out.shape[0]] = jnp.zeros((y_out.shape[0] - rows - tall, LANES), jnp.float32)


def reversed_lanes(x):
    index = LANES - 1 - lane_index(x.shape[0])
    return jnp.take_along_axis(x, index, axis=1, mode="promise_in_bounds")


def fold_kernel(levels, used, place, *refs):
    blocks, (out, placed, arrived) = refs[:-3], refs[-3:]
    lon_even = lax.rem(lax.axis_index("lon"), 2) == 0
    copy = pltpu.make_async_copy(place, placed, arrived)
    copy.start()
    arrays, rows, wide = out.shape
    cols = wide - LANES
    tiles_across = cols // LANES
    band = (arrays + 2) * TILE
    copy.wait()
    offset = placed[0, 1]
    span = 3 * cols
    far = lane_index(rows)

    for k in range(arrays):
        east_face = levels <= k < 2 * levels
        north_face = 2 * levels <= k < 3 * levels
        pieces = []
        for even, odd in used:
            for c in range(tiles_across - 1, -1, -1):
                main_at = c * band + k * TILE
                few_at = c * band + (arrays + k // 4) * TILE
                main, few = (
                    jnp.where(lon_even, blocks[even][at : at + TILE], blocks[odd][at : at + TILE])
                    for at in (main_at, few_at)
                )
                few = pltpu.roll(few, (TILE - 2 - 2 * (k % 4)) % TILE, 0)
                pieces.append(reversed_lanes(jnp.concatenate([few, main], axis=0)))
        shift = offset + span - cols + (0 if east_face else 1)
        turned = pltpu.roll(jnp.concatenate(pieces, axis=1), shift, 1)
        beyond = turned[:, cols : cols + LANES]
        before = turned[:, span - LANES :]
        side = jnp.where(far < ITERS, beyond, jnp.where(far >= LANES - ITERS, before, 0.0))
        mirrored = jnp.concatenate([turned[:, :cols], side], axis=1)
        skip = 1 if north_face else 0
        for row in range(rows - 1):
            source = max(rows - 1 - skip - row, 0)
            out[k, row : row + 1] = mirrored[source : source + 1]
        out[k, rows - 1 : rows] = mirrored[rows - 1 : rows]


def steps_kernel(levels, own, x_out, x_in, y_in, area, root, mirrored, out, ext):
    arrays, rows, cols = own.shape
    wide, tall = cols + LANES, 3 * rows
    tiles_across = cols // LANES
    band = (arrays + 2) * TILE
    data = band * tiles_across
    edge = (x_in.shape[0] - data) // 4
    lat = lax.axis_index("lat")
    lat_even = lax.rem(lat, 2) == 0
    at_top = lat == lax.axis_size("lat") - 1
    below_top = lat == lax.axis_size("lat") - 2
    lane = lane_index()

    def put_sides(start, from_east, from_west):
        for k, t, row, at in slots(arrays):
            here = slice(row * TILE, (row + 1) * TILE)
            east = pltpu.roll(from_east[here], (-at) % LANES, 1)
            west = pltpu.roll(from_west[here], (LANES - ITERS - at) % LANES, 1)
            side = jnp.where(lane < ITERS, east, jnp.where(lane >= LANES - ITERS, west, 0.0))
            ext[k, start + t * TILE : start + (t + 1) * TILE, cols:wide] = side

    def put_rows(start, main, spare, lift_base, rows_of):
        for c in range(tiles_across):
            at = slice(c * LANES, (c + 1) * LANES)
            for k in range(arrays):
                base = c * band
                ext[k, start + main * TILE : start + (main + 1) * TILE, at] = rows_of(base + k * TILE)
                few = rows_of(base + (arrays + k // 4) * TILE)
                lift = (lift_base - 2 * (k % 4)) % TILE
                ext[k, start + spare * TILE : start + (spare + 1) * TILE, at] = pltpu.roll(few, lift, 0)

    for k in range(arrays):
        ext[k, rows : 2 * rows, 0:cols] = own[k]
    def part(held, at):
        return held[data + at * edge : data + (at + 1) * edge]

    x_east, x_west = part(x_in, 0), part(x_in, 2)
    y_east, y_west = part(y_in, 0), part(y_in, 1)
    put_sides(
        rows,
        jnp.where(at_top, part(x_in, 1), part(x_out, 0)),
        jnp.where(at_top, part(x_in, 3), part(x_out, 2)),
    )

    def south_rows(at):
        return jnp.where(lat_even, y_in[at : at + TILE], x_in[at : at + TILE])

    def north_rows(at):
        return jnp.where(lat_even, x_in[at : at + TILE], y_in[at : at + TILE])

    put_rows(0, 1, 0, TILE - 2, south_rows)
    put_sides(0, jnp.where(lat_even, y_east, x_east), jnp.where(lat_even, y_west, x_west))

    @pl.when(jnp.logical_not(at_top))
    def _():
        put_rows(2 * rows, 0, 1, 0, north_rows)
        put_sides(
            2 * rows,
            jnp.where(below_top, part(x_out, 1), jnp.where(lat_even, x_east, y_east)),
            jnp.where(below_top, part(x_out, 3), jnp.where(lat_even, x_west, y_west)),
        )

    @pl.when(at_top)
    def _():
        for k in range(arrays):
            ext[k, 2 * rows : 3 * rows] = mirrored[k]
        for k in range(2 * levels, 3 * levels):
            face = ext[k, 2 * rows - 1 : 2 * rows]
            ext[k, 2 * rows - 1 : 2 * rows] = 0.5 * (face + mirrored[k, rows - 1 : rows])

    def east_of(x):
        return pltpu.roll(x, wide - 1, 1)

    def west_of(x):
        return pltpu.roll(x, 1, 1)

    def north_of(x):
        return pltpu.roll(x, x.shape[0] - 1, 0)

    def south_of(x):
        return pltpu.roll(x, 1, 0)

    weight = ext[3 * levels]
    sea = jnp.where(weight > 0.0, 1.0, 0.0)
    sea_east = sea * east_of(sea)
    sea_north = sea * north_of(sea)
    inner = slice(TILE, tall - TILE)
    coefs, values = [], []
    for level in range(levels):
        east = ext[levels + level] * sea_east
        north = ext[2 * levels + level] * sea_north
        west, south = west_of(east), south_of(north)
        rest = 1.0 - weight * ((east + west) + (north + south))
        coefs.append([rest] + [weight * x for x in (east, west, north, south)])
        values.append(weight * ext[level])
    for turn in range(ITERS):
        for level in range(levels):
            u = values[level]
            rest, east, west, north, south = coefs[level]
            u = (rest * u + (east * east_of(u) + west * west_of(u))) + (
                north * north_of(u) + south * south_of(u)
            )
            if turn == 1:
                u = u[inner]
                coefs[level] = [x[inner] for x in coefs[level]]
            values[level] = u
    start = rows - TILE
    own_weight = weight[rows : 2 * rows, :cols]
    for level in range(levels):
        u = values[level][start : start + rows, :cols]
        state = jnp.where(own_weight > 0.0, u * area[...], own[level])
        out[level] = state / root[...]


VMEM = pl.BlockSpec(memory_space=pltpu.VMEM)
SMEM = pl.BlockSpec(memory_space=pltpu.SMEM)
ANY = pl.BlockSpec(memory_space=pl.ANY)
HBM = pl.BlockSpec(memory_space=pltpu.HBM)
PARAMS = pltpu.CompilerParams(vmem_limit_bytes=8 * 1024 * 1024)


def per_device(gradient, norm_factor, diff_east, diff_north, cell_area, sea_mask, partner):
    levels, rows, cols = gradient.shape
    arrays = 3 * levels + 1
    lon_count, lat_count = lax.axis_size("lon"), lax.axis_size("lat")

    def held(*shape):
        return jax.ShapeDtypeStruct(shape, jnp.float32)

    inputs = (gradient, norm_factor, diff_east, diff_north, cell_area, sea_mask)
    edge = (slots(arrays)[-1][2] + 1) * TILE
    data = (arrays + 2) * TILE * (cols // LANES)
    def flat(lon, lat):
        return (lon % lon_count) * lat_count + lat

    top = lat_count - 1
    around = range(lon_count)

    def swap(pairs):
        return [pair for a, b in pairs for pair in ((a, b), (b, a))]

    def sent(start, step):
        return [(flat(p, i), flat(p + step, i)) for p in around[start::2] for i in range(top)]

    def lat_swap(start, parity):
        return swap(
            [(flat(p, i), flat(p, i + 1)) for p in around[parity::2] for i in range(start, top, 2)]
        )

    def mirror(total):
        return [(flat(total - p, top), flat(p, top)) for p in around]

    packed_shapes = (
        held(arrays, rows, cols),
        held(2 * edge, LANES),
        held(data, LANES),
        held(data, LANES),
        held(rows, cols),
        held(rows, cols),
    )
    joined_shapes = (held(2 * edge, LANES),) * 2
    odd = lax.rem(lax.axis_index("lon"), 2)

    def join(edges, mate):
        return pl.pallas_call(
            join_kernel,
            out_shape=joined_shapes,
            in_specs=[VMEM] * 2,
            out_specs=(VMEM,) * 2,
            compiler_params=PARAMS,
        )(edges, mate)

    def in_hbm(*arrays):
        return [pltpu.with_memory_space_constraint(x, pltpu.HBM) for x in arrays]

    buffers = [pltpu.VMEM(x.shape, x.dtype) for x in inputs]
    *early_held, place = pl.pallas_call(
        pack_kernel,
        out_shape=packed_shapes + (jax.ShapeDtypeStruct((TILE, LANES), jnp.int32),),
        in_specs=[HBM] * 7,
        out_specs=(VMEM,) * 7,
        scratch_shapes=buffers
        + [pltpu.SMEM((LANES,), jnp.int32), pltpu.SemaphoreType.DMA((7,))],
        compiler_params=PARAMS,
    )(*in_hbm(partner, *inputs))

    def mates(parity):
        return [(flat(p, top), flat(p, top - 1)) for p in around[parity::2]]

    def fetch(edges):
        return join(edges, lax.ppermute(edges, AXES, mates(1)))

    def no_fetch(edges):
        return join(edges, edges)

    near_top = lax.axis_index("lat") >= top - 1
    edges = early_held[1]
    to_east, to_west = lax.switch(
        (near_top & (odd == 1)).astype(jnp.int32), [no_fetch, fetch], edges
    )
    even_east = lax.ppermute(to_west, AXES, sent(1, -1))
    even_west = lax.ppermute(to_east, AXES, sent(1, 1))

    def late_fetch(edges):
        return after(lax.ppermute(edges, AXES, mates(0)))

    late_mate = lax.switch(
        (near_top & (odd == 0)).astype(jnp.int32), [after, late_fetch], after(edges, to_west)
    )
    late_held = pl.pallas_call(
        late_pack_kernel,
        out_shape=packed_shapes,
        in_specs=[HBM] * 6 + [VMEM] * 6 + [ANY],
        out_specs=(VMEM,) * 6,
        scratch_shapes=buffers + [pltpu.SemaphoreType.DMA((6,))],
        compiler_params=PARAMS,
    )(*in_hbm(*inputs), *early_held, late_mate)
    mirrored_shape = (arrays, rows, cols + LANES)

    def fold(total, third):
        totals = [total, total - 1] + [total - 2] * third
        steps = [(n, None) for n in sorted(range(len(totals)), key=lambda n: totals[n] % 2)]
        used = [[0, 0] for _ in range(3)]
        for at, (n, parity) in enumerate(steps):
            for side in (0, 1):
                if parity in (None, side):
                    used[n][side] = at

        def run(x, place):
            blocks = []
            for n, parity in steps:
                pairs = [
                    (flat(totals[n] - p, top), flat(p, top))
                    for p in around
                    if parity in (None, p % 2)
                ]
                blocks.append(lax.ppermute(x, AXES, pairs))
            return pl.pallas_call(
                functools.partial(fold_kernel, levels, used),
                out_shape=held(*mirrored_shape),
                in_specs=[ANY] + [VMEM] * len(blocks),
                out_specs=VMEM,
                scratch_shapes=[pltpu.SMEM((TILE, LANES), jnp.int32), pltpu.SemaphoreType.DMA],
                compiler_params=PARAMS,
            )(place, *blocks)

        return run

    def at_top(rows_held, place):
        folds = [fold(total, third) for total in around for third in (False, True)]
        return after(lax.switch(place[0, 0], folds, rows_held, place))

    def below(rows_held, place):
        return jnp.zeros(mirrored_shape, jnp.float32)

    mirrored = lax.switch(
        (lax.axis_index("lat") == top).astype(jnp.int32), [below, at_top], early_held[3], after(place, late_mate)
    )

    def near(held_here, east, west):
        _, _, x_rows, y_rows, _, _ = held_here
        return pl.pallas_call(
            near_kernel,
            out_shape=(held(data + 4 * edge, LANES), held(data + 4 * edge + TILE, LANES)),
            in_specs=[VMEM] * 4,
            out_specs=(VMEM,) * 2,
            compiler_params=PARAMS,
        )(x_rows, y_rows, east, west)

    def steps(held_here, x_out, x_in, y_in):
        block, _, _, _, area, root = held_here
        return pl.pallas_call(
            functools.partial(steps_kernel, levels),
            out_shape=held(levels, rows, cols),
            in_specs=[VMEM] * 7,
            out_specs=VMEM,
            scratch_shapes=[pltpu.VMEM((arrays, 3 * rows, cols + LANES), jnp.float32)],
            compiler_params=PARAMS,
        )(block, x_out, x_in, y_in, area, root, mirrored)

    x_out, y_out = near(late_held, even_east, even_west)
    go_east, go_west = join(after(late_held[1], y_out, mirrored), late_mate)
    y_in = lax.ppermute(y_out, AXES, lat_swap(1, 0))
    odd_west = lax.ppermute(go_east, AXES, sent(0, 1))
    odd_east = lax.ppermute(go_west, AXES, sent(0, -1))
    x_in = lax.ppermute(after(x_out, odd_west, odd_east), AXES, lat_swap(0, 0))

    def even_steps(x_out, x_in, y_in, east, west):
        return steps(late_held, x_out, x_in, y_in)

    def odd_steps(x_out, x_in, y_in, east, west):
        x_out, y_out = near(early_held, east, west)
        y_in = lax.ppermute(y_out, AXES, lat_swap(1, 1))
        x_in = lax.ppermute(x_out, AXES, lat_swap(0, 1))
        return steps(early_held, x_out, x_in, y_in)

    return lax.switch(
        odd,
        [even_steps, odd_steps],
        x_out,
        x_in,
        y_in,
        odd_east,
        odd_west,
    )


def solution(mesh):
    return jax.shard_map(
        per_device,
        mesh=mesh,
        in_specs=(
            P(None, "lat", "lon"),
            P(None, "lat", "lon"),
            P(None, "lat", "lon"),
            P(None, "lat", "lon"),
            P("lat", "lon"),
            P("lat", "lon"),
            P(),
        ),
        out_specs=P(None, "lat", "lon"),
        check_vma=False,
    )
```
